128 devices in a mesh: axial: 32 (over y, x, core), theta: 4 (over z).
Axes of the slice: x: 4, y: 4, z: 4, core: 2. Of those that a mesh axis runs over, the one named last changes fastest.
Arguments:
- rhs_field: float32 [16, 64, 32, 320], P('theta', 'axial'), may hold values from -6 to 6
- diag_inv: float32 [16, 64, 320, 320], P('theta', 'axial'), may hold values from -0.5 to 2
- lower_block: float32 [16, 64, 320, 320], P('theta', 'axial'), may hold values from -2 to 0.5
- upper_block: float32 [16, 64, 320, 320], P('theta', 'axial'), may hold values from -2 to 0.5
- proj_table: float32 [16, 80, 80], replicated, may hold values from -0.5 to 0.5
- intersection_list: int32 [16, 2], P('theta'), may hold values from 0 to 15
- proj_index: int32 [16, 2], P('theta'), may hold values from 0 to 15
- angle_step: int32 [1], replicated, may hold values from 0 to 15
Outputs:
- solution: float32 [16, 64, 32, 320], P('theta', 'axial')
- mortar: float32 [32, 16, 2560], P('axial', 'theta')
The draws below stay inside these ranges and needn't reach their ends.
All inputs are finite; a program needn't handle non-finite values.
Results may differ from the reference program's by a relative error of at most 0.0002.
Values sent between devices are 32-bit elements; how exact they have to be, the bound alone decides.
A program may use at most 64 MiB of HBM per device.

```python
import math
import jax
import jax.numpy as jnp
from jax import lax

B = 320
FACE = 80
ELEM_DEV = 2
VECS = 32
NPROJ = 16
INTERSECTIONS = 2
ELEMENTS_PER_LINE = 64
LINE_COUNT_TOTAL = 16
N_AXIAL = 32


def line_rates(key, salt_value):
    base_key = jax.random.fold_in(key, salt_value)
    random_keys = jax.random.split(base_key, 5)
    slow_share = 0.5
    slow_mask = jax.random.uniform(random_keys[0], (LINE_COUNT_TOTAL, B)) < slow_share
    slow_rate = jax.random.uniform(random_keys[1], (LINE_COUNT_TOTAL, B), minval=0.9, maxval=0.96)
    fast_rate = jnp.exp(jax.random.uniform(random_keys[2], (LINE_COUNT_TOTAL, B), minval=math.log(0.05), maxval=math.log(0.5)))
    base_rate = jnp.where(slow_mask, slow_rate, fast_rate)
    jitter = jax.random.uniform(random_keys[3], (LINE_COUNT_TOTAL, ELEMENTS_PER_LINE, B), minval=0.98, maxval=1.02)
    surge_events = jax.random.randint(random_keys[4], (LINE_COUNT_TOTAL, 3), 0, ELEMENTS_PER_LINE)
    element_numbers = jnp.arange(ELEMENTS_PER_LINE, dtype=jnp.int32)
    surge_flag = jnp.any(surge_events[:, None, :] == element_numbers[None, :, None], axis=-1)
    sweep_rates = jnp.minimum(base_rate[:, None, :] * jitter, 0.97)
    return sweep_rates * jnp.where(surge_flag[:, :, None], 0.6, 1.0)


def diag_scale(key):
    return jnp.exp(jax.random.uniform(jax.random.fold_in(key, 11), (LINE_COUNT_TOTAL, ELEMENTS_PER_LINE, B), minval=math.log(0.7), maxval=math.log(1.4)))


def block_noise(key, salt_value):
    noise = jax.random.normal(jax.random.fold_in(key, salt_value), (LINE_COUNT_TOTAL, ELEMENTS_PER_LINE, B, B), jnp.float32)
    return jnp.clip(noise, -4.0, 4.0) * (0.2 / math.sqrt(B))


def draw_diag_inv(key, part):
    scales = diag_scale(key)
    identity = jnp.eye(B, dtype=jnp.float32)
    return scales[..., None] * identity + block_noise(key, 21) * scales[..., None]


def draw_lower_block(key, part):
    ratio = line_rates(key, 31) / diag_scale(key)
    identity = jnp.eye(B, dtype=jnp.float32)
    return -(ratio[..., None] * identity + block_noise(key, 41) * ratio[..., None])


def draw_upper_block(key, part):
    ratio = line_rates(key, 51) / diag_scale(key)
    identity = jnp.eye(B, dtype=jnp.float32)
    return -(ratio[..., None] * identity + block_noise(key, 61) * ratio[..., None])


def touch_ends(values, stream_key, least, largest):
    place = [jax.random.randint(jax.random.fold_in(stream_key, axis), (), 0, length) for axis, length in enumerate(values.shape)]
    main_axis = values.shape.index(max(values.shape))
    neighbour = place[:main_axis] + [(place[main_axis] + 1) % values.shape[main_axis]] + place[main_axis + 1:]
    return values.at[tuple(place)].set(least).at[tuple(neighbour)].set(largest)


def block_scale(stream_key, shape, shards, low, high):
    gain = 1.0
    for dim, shards_of in shards:
        heights = jax.random.uniform(jax.random.fold_in(jax.random.fold_in(stream_key, 6), dim), (shards_of,), jnp.float32, low / len(shards), high / len(shards))
        gain = gain * jnp.repeat(jnp.exp(heights), shape[dim] // shards_of).reshape((-1,) + (1,) * (len(shape) - 1 - dim))
    return gain


def normal_values(key, extent, width, bound, cuts=(), kind=jnp.bfloat16):
    level = block_scale(key, extent, cuts, -0.22, 0.18) if cuts else 1.0
    array = jax.random.normal(key, extent, jnp.float32) * width * level
    return jnp.minimum(jnp.maximum(array, -bound), bound).astype(kind)


def setup_inputs(seed: int = 0) -> dict:
    splits = jax.random.split(jax.random.key(seed), 9)
    rhs_field = normal_values(splits[0], (LINE_COUNT_TOTAL, ELEMENTS_PER_LINE, VECS, B), 1.0, 6.0, ((0, 4), (1, 32)), jnp.float32)
    diag_inv = draw_diag_inv(jax.random.fold_in(splits[8], 71), 0)
    lower_block = draw_lower_block(jax.random.fold_in(splits[8], 71), 0)
    upper_block = draw_upper_block(jax.random.fold_in(splits[8], 71), 0)
    proj_table = normal_values(splits[4], (NPROJ, FACE, FACE), (2 * FACE) ** -0.5, 0.5, (), jnp.float32)
    intersection_list = touch_ends(jax.random.randint(splits[5], (LINE_COUNT_TOTAL, INTERSECTIONS), 0, LINE_COUNT_TOTAL), jax.random.fold_in(splits[5], 1), 0, LINE_COUNT_TOTAL - 1).astype(jnp.int32)
    proj_index = touch_ends(jax.random.randint(splits[6], (LINE_COUNT_TOTAL, INTERSECTIONS), 0, NPROJ), jax.random.fold_in(splits[6], 1), 0, NPROJ - 1).astype(jnp.int32)
    angle_step = jax.random.randint(splits[7], (1,), 0, LINE_COUNT_TOTAL).astype(jnp.int32)
    return dict(rhs_field=rhs_field, diag_inv=diag_inv, lower_block=lower_block, upper_block=upper_block, proj_table=proj_table, intersection_list=intersection_list, proj_index=proj_index, angle_step=angle_step)


def product(blocks, vectors):
    return jnp.einsum('lbc,lvc->lvb', blocks, vectors, precision=lax.Precision.HIGHEST)


def reference(rhs_field, diag_inv, lower_block, upper_block, proj_table, intersection_list, proj_index, angle_step):
    def select_element(source, element):
        return lax.dynamic_index_in_dim(source, element, 1, keepdims=False)

    def forward(previous, element):
        inner = select_element(rhs_field, element) - product(select_element(lower_block, element), previous)
        current = product(select_element(diag_inv, element), inner)
        return current, current

    zero_state = jnp.zeros((LINE_COUNT_TOTAL, VECS, B), jnp.float32)
    element_numbers = jnp.arange(ELEMENTS_PER_LINE, dtype=jnp.int32)
    _, swept = lax.scan(forward, zero_state, element_numbers)

    def backward(following, element):
        coupled = product(select_element(upper_block, element), following)
        current = lax.dynamic_index_in_dim(swept, element, 0, keepdims=False) - product(select_element(diag_inv, element), coupled)
        return current, current

    _, solved = lax.scan(backward, zero_state, element_numbers, reverse=True)
    solution = jnp.transpose(solved, (1, 0, 2, 3))
    traces = solution[:, ELEM_DEV - 1::ELEM_DEV, :, B - FACE:]
    sources = ((intersection_list + angle_step[0]) % LINE_COUNT_TOTAL).astype(jnp.int32)
    picked = traces[sources]
    one_hot = jax.nn.one_hot(proj_index, NPROJ, dtype=jnp.float32)
    chosen = jnp.einsum('gkp,pfh->gkfh', one_hot, proj_table, precision=lax.Precision.HIGHEST)
    mortar = jnp.einsum('gkfh,gkavh->agvf', chosen, picked, precision=lax.Precision.HIGHEST)
    return solution, mortar.reshape(N_AXIAL, LINE_COUNT_TOTAL, VECS * FACE)
```

```python
import jax
import jax.numpy as jnp
from jax import lax
from jax.experimental import pallas as pl
from jax.experimental.pallas import tpu as pltpu
from jax.sharding import PartitionSpec as P

MESH = pl.DeviceIdType.MESH
F32 = jnp.float32
BF16 = jnp.bfloat16
B = 320
V = 32
FACE = 80
LINES = 4


def split(value):
    high = value.astype(BF16)
    return high, (value - high.astype(F32)).astype(BF16)


def dot(a, b):
    return lax.dot_general(a, b, (((1,), (0,)), ((), ())), preferred_element_type=F32)


def dot_nt(a, b):
    return lax.dot_general(a, b, (((1,), (1,)), ((), ())), preferred_element_type=F32)


def product(a, b):
    return dot(a[0], b[0]) + dot(a[1], b[0]) + dot(a[0], b[1])


def apply(matrix, vectors):
    high, low = split(vectors)
    both = dot_nt(jnp.concatenate([high, low], 0), matrix[0])
    rows = vectors.shape[0]
    return both[:rows] + both[rows:] + dot_nt(high, matrix[1])


def apply_turned(matrix, vectors):
    high, low = split(vectors)
    both = dot(jnp.concatenate([high, low], 0), matrix[0])
    rows = vectors.shape[0]
    return both[:rows] + both[rows:] + dot(high, matrix[1])


def kernel(
    rhs_hbm, diag_hbm, lower_hbm, upper_hbm, proj_ref, list_ref, index_ref, angle_ref,
    out_ref, mortar_ref,
    diag, lower, upper, rhs,
    a_hl, g_hl, t_hl, w_hl, t_f, w_f, e_f, b_v, c_v, d_v,
    t_p, w_p, e_p, c_p, d_p,
    t_c, w_c, e_c, c_c, d_c,
    t_g, w_g, e_g, c_g, d_g,
    s_hop, x_hop, s_st, x_st, hop_st,
    s_in, x_in, s_0, s_1, u_0,
    tr_st, tr_all,
    load_sem, pair_s, pair_r, home_s, home_r, hop_s, hop_r,
    scat_s, sin_r, xin_r, core_s, tr_s, tr_r,
):
    axial = lax.axis_index("axial")
    theta = lax.axis_index("theta")
    core = lax.rem(axial, 2)
    x = lax.rem(axial // 2, 4)
    y = axial // 8
    other = 1 - core

    def at(row, chip, which):
        return ((row * 4 + chip) * 2 + which, theta)

    def remote(src, dst, send, recv, device):
        return pltpu.make_async_remote_copy(
            src_ref=src, dst_ref=dst, send_sem=send, recv_sem=recv,
            device_id=device, device_id_type=MESH,
        )

    barrier = pltpu.get_barrier_semaphore()

    def greet(device):
        pl.semaphore_signal(barrier, inc=1, device_id=device, device_id_type=MESH)

    for step in range(1, 8):
        greet((y * 8 + lax.rem(axial + step, 8), theta))
    greet((lax.rem(axial + 8, 32), theta))
    greet((lax.rem(axial + 24, 32), theta))
    for step in range(1, 4):
        greet((axial, lax.rem(theta + step, 4)))

    def load(which, line):
        src, dst = ((diag_hbm, diag), (lower_hbm, lower), (upper_hbm, upper), (rhs_hbm, rhs))[which]
        return pltpu.make_async_copy(src.at[line], dst.at[line], load_sem.at[which, line])

    order = [lax.rem(2 * other + i, 4) for i in range(4)]
    for line in order:
        load(0, line).start()
        load(1, line).start()
        load(3, line).start()
    for line in order:
        load(2, line).start()

    def whole(ref, *where):
        return ref[(*where, 0)], ref[(*where, 1)]

    def keep(ref, pair, *where):
        ref[(*where, 0)] = pair[0]
        ref[(*where, 1)] = pair[1]

    def first_maps(line):
        load(0, line).wait()
        load(1, line).wait()
        load(3, line).wait()
        for e in range(2):
            inverse = split(diag[line, e])
            keep(a_hl, split(product(inverse, split(lower[line, e]))), line, e)
            b_v[line, e] = apply(inverse, rhs[line, e])
        second = whole(a_hl, line, 1)
        across = product(second, whole(a_hl, line, 0))
        t_f[line] = across
        keep(t_hl, split(across), line)
        c_v[line] = b_v[line, 1] - apply(second, b_v[line, 0])

    def second_maps(line):
        load(2, line).wait()
        for e in range(2):
            keep(g_hl, split(product(split(diag[line, e]), split(upper[line, e]))), line, e)
        first = whole(g_hl, line, 0)
        across = product(first, whole(g_hl, line, 1))
        w_f[line] = across
        keep(w_hl, split(across), line)
        e_f[line] = -(
            a_hl[line, 0, 0].astype(F32) + a_hl[line, 0, 1].astype(F32)
        ) - product(first, whole(t_hl, line))
        d_v[line] = b_v[line, 0] - apply(first, c_v[line])

    def to_pair(kind, i):
        line = 2 * other + i
        src, dst = ((t_f, t_p), (c_v, c_p), (w_f, w_p), (e_f, e_p), (d_v, d_p))[kind]
        return remote(
            src.at[line], dst.at[i], pair_s.at[kind, i], pair_r.at[kind, i], at(y, x, other)
        )

    gathered = ((t_c, t_g), (c_c, c_g), (w_c, w_g), (e_c, e_g), (d_c, d_g))

    def to_home(kind, i, slot):
        src, dst = gathered[kind]
        return remote(
            src.at[i], dst.at[slot], home_s.at[kind, i], home_r.at[kind, slot],
            at(y, 2 * core + i, core),
        )

    def send_home(kinds, i):
        mine = x == 2 * core + i

        @pl.when(jnp.logical_not(mine))
        def _():
            for kind in kinds:
                to_home(kind, i, x).start()

        @pl.when(mine)
        def _():
            for kind in kinds:
                src, dst = gathered[kind]
                dst[x] = src[i]

    def pair_first(i, carry):
        first_maps(2 * other + i)

        @pl.when(i == 0)
        def _():
            pl.semaphore_wait(barrier, 12)

        to_pair(0, i).start()
        to_pair(1, i).start()
        return carry

    lax.fori_loop(0, 2, pair_first, 0)

    def pick(own, given):
        mine = core == 0
        return jnp.where(mine, own, given), jnp.where(mine, given, own)

    def own_first(i, carry):
        line = 2 * core + i
        first_maps(line)
        to_pair(0, i).wait_recv()
        to_pair(1, i).wait_recv()
        t_a, t_b = pick(t_f[line], t_p[i])
        c_a, c_b = pick(c_v[line], c_p[i])
        t_b = split(t_b)
        t_c[i] = product(t_b, split(t_a))
        c_c[i] = c_b + apply(t_b, c_a)
        send_home((0, 1), i)
        return carry

    lax.fori_loop(0, 2, own_first, 0)

    def pair_second(i, carry):
        second_maps(2 * other + i)
        for kind in (2, 3, 4):
            to_pair(kind, i).start()
        return carry

    lax.fori_loop(0, 2, pair_second, 0)

    def own_second(i, carry):
        line = 2 * core + i
        second_maps(line)
        for kind in (2, 3, 4):
            to_pair(kind, i).wait_recv()
        t_a, _ = pick(t_f[line], t_p[i])
        c_a, _ = pick(c_v[line], c_p[i])
        w_a, w_b = pick(w_f[line], w_p[i])
        e_a, e_b = pick(e_f[line], e_p[i])
        d_a, d_b = pick(d_v[line], d_p[i])
        w_a = split(w_a)
        e_b = split(e_b)
        w_c[i] = product(w_a, split(w_b))
        e_c[i] = e_a + product(w_a, split(product(e_b, split(t_a))))
        d_c[i] = d_a + apply(w_a, d_b + apply(e_b, c_a))
        send_home((2, 3, 4), i)
        return carry

    lax.fori_loop(0, 2, own_second, 0)

    is_home = x // 2 == core
    zero = jnp.zeros((V, B), F32)

    def arrived(kinds, slot):
        @pl.when(x != slot)
        def _():
            for kind in kinds:
                to_home(kind, 0, slot).wait_recv()

    def hop(way):
        src, dst, row = ((hop_st.at[0], s_hop, y + 1), (hop_st.at[1], x_hop, y - 1))[way]
        return remote(src, dst, hop_s.at[way], hop_r.at[way], at(row, x, core))

    def scatter(way, chip):
        src, dst, sem = ((s_st, s_in, sin_r), (x_st, x_in, xin_r))[way]
        return remote(src.at[chip], dst.at[x], scat_s.at[way, chip], sem.at[x], at(y, chip, way))

    def spread(way, chip, value):
        src, dst = ((s_st, s_in), (x_st, x_in))[way]
        src[chip] = value
        mine = jnp.logical_and(x == chip, core == way)

        @pl.when(jnp.logical_not(mine))
        def _():
            scatter(way, chip).start()

        @pl.when(mine)
        def _():
            dst[x] = value

    def home_forward():
        @pl.when(y == 0)
        def _():
            s_hop[...] = zero

        @pl.when(y > 0)
        def _():
            hop(0).wait_recv()

        state = s_hop[...]
        for chip in range(4):
            arrived((0, 1), chip)
            spread(0, chip, state)
            state = c_g[chip] + apply_turned(split(t_g[chip].T), state)
        hop_st[0] = state

        @pl.when(y < 3)
        def _():
            hop(0).start()

        for chip in range(4):
            arrived((3, 4), chip)
            d_g[chip] = d_g[chip] + apply(split(e_g[chip]), s_st[chip])

    def home_backward():
        @pl.when(y == 3)
        def _():
            x_hop[...] = zero

        @pl.when(y < 3)
        def _():
            hop(1).wait_recv()

        state = x_hop[...]
        for chip in (3, 2, 1, 0):
            arrived((2,), chip)
            spread(1, chip, state)
            state = d_g[chip] + apply_turned(split(w_g[chip].T), state)
        hop_st[1] = state

        @pl.when(y > 0)
        def _():
            hop(1).start()

    def to_core(line):
        forward = remote(
            s_1.at[line], s_in.at[line], core_s.at[line], sin_r.at[line], at(y, x, other)
        )
        back = remote(
            out_ref.at[line, 0], x_in.at[line], core_s.at[line], xin_r.at[line], at(y, x, other)
        )
        return forward, back

    def wait_state(line):
        mine = jnp.logical_and(is_home, jnp.logical_and(x == line, core == 0))

        @pl.when(jnp.logical_not(mine))
        def _():
            to_core(line)[0].wait_recv()

    def wait_solution(line):
        mine = jnp.logical_and(is_home, jnp.logical_and(x == line, core == 1))

        @pl.when(jnp.logical_not(mine))
        def _():
            to_core(line)[1].wait_recv()

    def finish_forward():
        for line in range(LINES):
            wait_state(line)
            s_1[line] = c_v[line] + apply(whole(t_hl, line), s_in[line])

            @pl.when(core == 0)
            def _():
                to_core(line)[0].start()

        for line in range(LINES):
            s_0[line] = b_v[line, 0] - apply(whole(a_hl, line, 0), s_in[line])
            u_0[line] = s_0[line] - apply(whole(g_hl, line, 0), s_1[line])

    def solve_first(line):
        out_ref[line, 0] = u_0[line] + apply(whole(w_hl, line), x_in[line])

    def solve_last(line):
        value = s_1[line] - apply(whole(g_hl, line, 1), x_in[line])
        out_ref[line, 1] = value
        tr_st[line] = value[:, B - FACE :]

    def to_theta(step):
        return remote(
            tr_st, tr_all.at[pl.ds(4 * theta, 4)], tr_s.at[step], tr_r.at[step],
            (axial, lax.rem(theta + step, 4)),
        )

    @pl.when(is_home)
    def _():
        home_forward()

    @pl.when(jnp.logical_and(is_home, y == 3))
    def _():
        home_backward()

    finish_forward()

    @pl.when(jnp.logical_and(is_home, y < 3))
    def _():
        home_backward()

    @pl.when(core == 1)
    def _():
        for line in range(LINES):
            wait_solution(line)
            solve_first(line)
            to_core(line)[1].start()
        for line in range(LINES):
            solve_last(line)

    @pl.when(core == 0)
    def _():
        for line in range(LINES):
            wait_solution(line)
            solve_last(line)

    for step in range(1, 4):
        to_theta(step).start()
    tr_all[pl.ds(4 * theta, 4)] = tr_st[...]

    @pl.when(core == 0)
    def _():
        for line in range(LINES):
            solve_first(line)

    for step in range(1, 4):
        to_theta(step).wait_recv()

    for face in range(LINES):
        total = jnp.zeros((V, FACE), F32)
        for k in range(2):
            source = lax.rem(list_ref[face, k] + angle_ref[0], 16)
            total += apply(split(proj_ref[index_ref[face, k]]), tr_all[source])
        mortar_ref[face] = total

    for i in range(2):
        mine = x == 2 * core + i
        for kind in range(5):
            to_pair(kind, i).wait_send()

            @pl.when(jnp.logical_not(mine))
            def _():
                to_home(kind, i, x).wait_send()

    @pl.when(is_home)
    def _():
        for way in range(2):
            for chip in range(4):
                mine = jnp.logical_and(x == chip, core == way)

                @pl.when(jnp.logical_not(mine))
                def _():
                    scatter(way, chip).wait_send()

        @pl.when(y < 3)
        def _():
            hop(0).wait_send()

        @pl.when(y > 0)
        def _():
            hop(1).wait_send()

    for line in range(LINES):
        @pl.when(core == 0)
        def _():
            to_core(line)[0].wait_send()

        @pl.when(core == 1)
        def _():
            to_core(line)[1].wait_send()

    for step in range(1, 4):
        to_theta(step).wait_send()


def local(rhs, diag, lower, upper, proj, intersections, index, angle):
    def mats(*lead, kind=F32):
        return pltpu.VMEM((*lead, B, B), kind)

    def vecs(*lead):
        return pltpu.VMEM((*lead, V, B), F32)

    def sems(*shape):
        return pltpu.SemaphoreType.DMA(shape)

    anywhere = pl.BlockSpec(memory_space=pl.ANY)
    vmem = pl.BlockSpec(memory_space=pltpu.VMEM)
    smem = pl.BlockSpec(memory_space=pltpu.SMEM)
    result, mortar = pl.pallas_call(
        kernel,
        out_shape=(
            jax.ShapeDtypeStruct((LINES, 2, V, B), F32),
            jax.ShapeDtypeStruct((LINES, V, FACE), F32),
        ),
        in_specs=[anywhere] * 4 + [vmem] + [smem] * 3,
        out_specs=(vmem, vmem),
        scratch_shapes=[
            mats(4, 2), mats(4, 2), mats(4, 2), vecs(4, 2),
            mats(4, 2, 2, kind=BF16), mats(4, 2, 2, kind=BF16), mats(4, 2, kind=BF16), mats(4, 2, kind=BF16),
            mats(4), mats(4), mats(4), vecs(4, 2), vecs(4), vecs(4),
            mats(2), mats(2), mats(2), vecs(2), vecs(2),
            mats(2), mats(2), mats(2), vecs(2), vecs(2),
            mats(4), mats(4), mats(4), vecs(4), vecs(4),
            vecs(), vecs(), vecs(4), vecs(4), vecs(2),
            vecs(4), vecs(4), vecs(4), vecs(4), vecs(4),
            pltpu.VMEM((4, V, FACE), F32), pltpu.VMEM((16, V, FACE), F32),
            sems(4, 4), sems(5, 2), sems(5, 2), sems(5, 2), sems(5, 4), sems(2), sems(2),
            sems(2, 4), sems(4), sems(4), sems(4), sems(4), sems(4),
        ],
        compiler_params=pltpu.CompilerParams(
            collective_id=0, has_side_effects=True, vmem_limit_bytes=60 * 2**20
        ),
        cost_estimate=pl.CostEstimate(flops=10**10, bytes_accessed=10**7, transcendentals=0),
    )(rhs, diag, lower, upper, proj, intersections, index, angle)
    return result, mortar.reshape(1, LINES, V * FACE)


def solution(mesh):
    line = P("theta", "axial", None, None)
    return jax.shard_map(
        local,
        mesh=mesh,
        in_specs=(line, line, line, line, P(), P("theta", None), P("theta", None), P()),
        out_specs=(line, P("axial", "theta", None)),
        check_vma=False,
    )
```

```python
import jax
import jax.numpy as jnp
from jax import lax
from jax.experimental import pallas as pl
from jax.experimental.pallas import tpu as pltpu
from jax.sharding import PartitionSpec as P

MESH = pl.DeviceIdType.MESH
F32 = jnp.float32
BF16 = jnp.bfloat16
B = 320
V = 32
FACE = 80
LINES = 4


def split(value):
    high = value.astype(BF16)
    return high, (value - high.astype(F32)).astype(BF16)


def dot(a, b):
    return lax.dot_general(a, b, (((1,), (0,)), ((), ())), preferred_element_type=F32)


def dot_nt(a, b):
    return lax.dot_general(a, b, (((1,), (1,)), ((), ())), preferred_element_type=F32)


def product(a, b):
    return dot(a[0], b[0]) + dot(a[1], b[0]) + dot(a[0], b[1])


def apply(matrix, vectors):
    high, low = split(vectors)
    both = dot_nt(jnp.concatenate([high, low], 0), matrix[0])
    rows = vectors.shape[0]
    return both[:rows] + both[rows:] + dot_nt(high, matrix[1])


def apply_turned(matrix, vectors):
    high, low = split(vectors)
    both = dot(jnp.concatenate([high, low], 0), matrix[0])
    rows = vectors.shape[0]
    return both[:rows] + both[rows:] + dot(high, matrix[1])


def packed(value):
    rest = value[:, 256:]
    return jnp.concatenate(
        [value[:, :128], value[:, 128:256], jnp.concatenate([rest[:160], rest[160:]], 1)], 0
    )


def unpacked(value):
    rest = value[640:]
    return jnp.concatenate(
        [value[:320], value[320:640], jnp.concatenate([rest[:, :64], rest[:, 64:]], 0)], 1
    )


def kernel(
    rhs_hbm, diag_hbm, lower_hbm, upper_hbm, proj_ref, list_ref, index_ref, angle_ref,
    out_ref, mortar_ref,
    diag, lower, upper, rhs,
    a_hl, g_hl, t_hl, w_hl, t_f, w_f, e_f, b_v, c_v, d_v,
    t_p, w_p, e_p, c_p, d_p,
    t_c, w_c, e_hl, c_c, d_c,
    t_g, w_g, c_g, d_g, turned, s_chip,
    s_hop, x_hop, s_st, x_st, hop_st,
    s_in, x_in, s_0, s_1, u_0,
    tr_st, tr_all,
    load_sem, pair_s, pair_r, home_s, home_r, hop_s, hop_r,
    scat_s, sin_r, xin_r, core_s, tr_s, tr_r, chip_s, chip_r,
):
    axial = lax.axis_index("axial")
    theta = lax.axis_index("theta")
    core = lax.rem(axial, 2)
    x = lax.rem(axial // 2, 4)
    y = axial // 8
    other = 1 - core

    def at(row, chip, which):
        return ((row * 4 + chip) * 2 + which, theta)

    def remote(src, dst, send, recv, device):
        return pltpu.make_async_remote_copy(
            src_ref=src, dst_ref=dst, send_sem=send, recv_sem=recv,
            device_id=device, device_id_type=MESH,
        )

    barrier = pltpu.get_barrier_semaphore()

    def greet(device):
        pl.semaphore_signal(barrier, inc=1, device_id=device, device_id_type=MESH)

    for step in range(1, 8):
        greet((y * 8 + lax.rem(axial + step, 8), theta))
    greet((lax.rem(axial + 8, 32), theta))
    greet((lax.rem(axial + 24, 32), theta))
    for step in range(1, 4):
        greet((axial, lax.rem(theta + step, 4)))

    def load(which, line):
        src, dst = ((diag_hbm, diag), (lower_hbm, lower), (upper_hbm, upper), (rhs_hbm, rhs))[which]
        return pltpu.make_async_copy(src.at[line], dst.at[line], load_sem.at[which, line])

    order = [2 * other, 2 * core, 2 * other + 1, 2 * core + 1]
    for line in order:
        load(0, line).start()
        load(1, line).start()
    for line in order:
        load(3, line).start()
    for line in order:
        load(2, line).start()

    def whole(ref, *where):
        return ref[(*where, 0)], ref[(*where, 1)]

    def keep(ref, pair, *where):
        ref[(*where, 0)] = pair[0]
        ref[(*where, 1)] = pair[1]

    def first_maps(line):
        load(0, line).wait()
        load(1, line).wait()
        for e in range(2):
            inverse = split(diag[line, e])
            keep(a_hl, split(product(inverse, split(lower[line, e]))), line, e)
        across = product(whole(a_hl, line, 1), whole(a_hl, line, 0))
        t_f[line] = across
        keep(t_hl, split(across), line)

    def first_vectors(line):
        load(3, line).wait()
        for e in range(2):
            b_v[line, e] = apply(split(diag[line, e]), rhs[line, e])
        c_v[line] = b_v[line, 1] - apply(whole(a_hl, line, 1), b_v[line, 0])

    def second_maps(line):
        load(2, line).wait()
        for e in range(2):
            keep(g_hl, split(product(split(diag[line, e]), split(upper[line, e]))), line, e)
        across = product(whole(g_hl, line, 0), whole(g_hl, line, 1))
        w_f[line] = across
        keep(w_hl, split(across), line)

    def third_maps(line):
        first = whole(g_hl, line, 0)
        e_f[line] = -(
            a_hl[line, 0, 0].astype(F32) + a_hl[line, 0, 1].astype(F32)
        ) - product(first, whole(t_hl, line))
        d_v[line] = b_v[line, 0] - apply(first, c_v[line])

    def to_pair(kind, i):
        line = 2 * other + i
        src, dst = ((t_f, t_p), (c_v, c_p), (w_f, w_p), (e_f, e_p), (d_v, d_p))[kind]
        return remote(
            src.at[line], dst.at[i], pair_s.at[kind, i], pair_r.at[kind, i], at(y, x, other)
        )

    gathered = ((t_c, t_g), (c_c, c_g), (w_c, w_g), None, (d_c, d_g))

    def to_home(kind, i, slot):
        src, dst = gathered[kind]
        return remote(
            src.at[i], dst.at[slot], home_s.at[kind, i], home_r.at[kind, slot],
            at(y, 2 * core + i, 1),
        )

    def send_home(kinds, i):
        mine = jnp.logical_and(x == 2 * core + i, core == 1)

        @pl.when(jnp.logical_not(mine))
        def _():
            for kind in kinds:
                to_home(kind, i, x).start()

        @pl.when(mine)
        def _():
            for kind in kinds:
                src, dst = gathered[kind]
                dst[x] = src[i]

    def both_first(i, carry):
        first_maps(2 * other + i)

        @pl.when(i == 0)
        def _():
            pl.semaphore_wait(barrier, 12)

        to_pair(0, i).start()
        first_maps(2 * core + i)
        return carry

    lax.fori_loop(0, 2, both_first, 0)

    def pick(own, given):
        mine = core == 0
        return jnp.where(mine, own, given), jnp.where(mine, given, own)

    def chip_first(i, carry):
        to_pair(0, i).wait_recv()
        t_a, t_b = pick(t_f[2 * core + i], t_p[i])
        t_c[i] = packed(product(split(t_b), split(t_a)))
        send_home((0,), i)
        return carry

    lax.fori_loop(0, 2, chip_first, 0)

    def pair_vectors(i, carry):
        first_vectors(2 * other + i)
        to_pair(1, i).start()
        return carry

    lax.fori_loop(0, 2, pair_vectors, 0)

    def own_vectors(i, carry):
        line = 2 * core + i
        first_vectors(line)
        to_pair(1, i).wait_recv()
        _, t_b = pick(t_f[line], t_p[i])
        c_a, c_b = pick(c_v[line], c_p[i])
        c_c[i] = c_b + apply(split(t_b), c_a)
        send_home((1,), i)
        return carry

    lax.fori_loop(0, 2, own_vectors, 0)

    is_home = core == 1
    zero = jnp.zeros((V, B), F32)

    def arrived(kinds, slot):
        @pl.when(jnp.logical_not(jnp.logical_and(x == slot, x // 2 == 1)))
        def _():
            for kind in kinds:
                to_home(kind, 0, slot).wait_recv()

    def hop(way):
        src, dst, row = ((hop_st.at[0], s_hop, y + 1), (hop_st.at[1], x_hop, y - 1))[way]
        return remote(src, dst, hop_s.at[way], hop_r.at[way], at(row, x, core))

    def scatter(way, chip):
        src, dst, sem = ((s_st, s_in, sin_r), (x_st, x_in, xin_r))[way]
        return remote(src.at[chip], dst.at[x], scat_s.at[way, chip], sem.at[x], at(y, chip, way))

    def to_chip(chip):
        return remote(
            s_st.at[chip], s_chip.at[jnp.maximum(x - 2, 0)], chip_s.at[chip],
            chip_r.at[jnp.maximum(x - 2, 0)], at(y, chip, 1),
        )

    def spread(way):
        for chip in range(4):
            src, dst = ((s_st, s_in), (x_st, x_in))[way]
            mine = jnp.logical_and(x == chip, core == way)

            @pl.when(jnp.logical_not(mine))
            def _():
                scatter(way, chip).start()

            @pl.when(mine)
            def _():
                dst[x] = src[chip]

    def home_forward():
        for chip in range(4):
            arrived((0, 1), chip)
            keep(turned, split(unpacked(t_g[chip]).T), chip)

        @pl.when(y == 0)
        def _():
            s_hop[...] = zero

        @pl.when(y > 0)
        def _():
            hop(0).wait_recv()

        state = s_hop[...]
        for chip in range(4):
            s_st[chip] = state
            state = c_g[chip] + apply_turned(whole(turned, chip), state)
        hop_st[0] = state

        @pl.when(y < 3)
        def _():
            hop(0).start()

        spread(0)
        for chip in range(4):
            @pl.when(jnp.logical_and(x > 1, x != chip))
            def _():
                to_chip(chip).start()

            @pl.when(jnp.logical_and(x > 1, x == chip))
            def _():
                s_chip[x - 2] = s_st[chip]

    def home_backward():
        for chip in (3, 2, 1, 0):
            arrived((2,), chip)
            keep(turned, split(unpacked(w_g[chip]).T), chip)
        for chip in (3, 2, 1, 0):
            arrived((4,), chip)

        @pl.when(y == 3)
        def _():
            x_hop[...] = zero

        @pl.when(y < 3)
        def _():
            hop(1).wait_recv()

        state = x_hop[...]
        for chip in (3, 2, 1, 0):
            x_st[chip] = state
            state = d_g[chip] + apply_turned(whole(turned, chip), state)
        hop_st[1] = state

        @pl.when(y > 0)
        def _():
            hop(1).start()

        spread(1)

    def home_at(row, here):
        @pl.when(jnp.logical_and(is_home, jnp.logical_and(y == row, here)))
        def _():
            home_forward()

    def pair_second(i, carry):
        second_maps(2 * other + i)
        to_pair(2, i).start()
        return carry

    lax.fori_loop(0, 2, pair_second, 0)

    def own_second(i, carry):
        home_at(0, i == 1)
        line = 2 * core + i
        second_maps(line)
        to_pair(2, i).wait_recv()
        w_a, w_b = pick(w_f[line], w_p[i])
        w_c[i] = packed(product(split(w_a), split(w_b)))
        send_home((2,), i)
        return carry

    lax.fori_loop(0, 2, own_second, 0)

    def pair_third(i, carry):
        home_at(1, i == 0)
        third_maps(2 * other + i)
        to_pair(3, i).start()
        to_pair(4, i).start()
        return carry

    lax.fori_loop(0, 2, pair_third, 0)

    def own_third(i, carry):
        home_at(2, i == 1)
        line = 2 * core + i
        third_maps(line)
        to_pair(3, i).wait_recv()
        to_pair(4, i).wait_recv()
        t_a, _ = pick(t_f[line], t_p[i])
        c_a, _ = pick(c_v[line], c_p[i])
        w_a, _ = pick(w_f[line], w_p[i])
        e_a, e_b = pick(e_f[line], e_p[i])
        d_a, d_b = pick(d_v[line], d_p[i])
        w_a = split(w_a)
        e_b = split(e_b)
        keep(e_hl, split(e_a + product(w_a, split(product(e_b, split(t_a))))), i)
        d_c[i] = d_a + apply(w_a, d_b + apply(e_b, c_a))
        return carry

    lax.fori_loop(0, 2, own_third, 0)
    home_at(3, True)

    def to_core(line):
        forward = remote(
            s_1.at[line], s_in.at[line], core_s.at[line], sin_r.at[line], at(y, x, other)
        )
        back = remote(
            out_ref.at[line, 0], x_in.at[line], core_s.at[line], xin_r.at[line], at(y, x, other)
        )
        return forward, back

    def chip_backward():
        for i in range(2):
            @pl.when(core == 0)
            def _():
                to_core(i)[0].wait_recv()
                d_c[i] = d_c[i] + apply(whole(e_hl, i), s_in[i])

            @pl.when(core == 1)
            def _():
                @pl.when(x != 2 + i)
                def _():
                    remote(
                        s_st.at[0], s_chip.at[i], chip_s.at[0], chip_r.at[i], at(y, x, other)
                    ).wait_recv()

                d_c[i] = d_c[i] + apply(whole(e_hl, i), s_chip[i])

            send_home((4,), i)

    def wait_solution(line):
        mine = jnp.logical_and(is_home, jnp.logical_and(x == line, core == 1))

        @pl.when(jnp.logical_not(mine))
        def _():
            to_core(line)[1].wait_recv()

    def finish_forward():
        for line in range(LINES):
            @pl.when(jnp.logical_or(core == 1, line > 1))
            def _():
                to_core(line)[0].wait_recv()

            s_1[line] = c_v[line] + apply(whole(t_hl, line), s_in[line])

            @pl.when(core == 0)
            def _():
                to_core(line)[0].start()

        for line in range(LINES):
            s_0[line] = b_v[line, 0] - apply(whole(a_hl, line, 0), s_in[line])
            u_0[line] = s_0[line] - apply(whole(g_hl, line, 0), s_1[line])

    def solve_first(line):
        out_ref[line, 0] = u_0[line] + apply(whole(w_hl, line), x_in[line])

    def solve_last(line):
        value = s_1[line] - apply(whole(g_hl, line, 1), x_in[line])
        out_ref[line, 1] = value
        tr_st[line] = value[:, B - FACE :]

    def to_theta(step):
        return remote(
            tr_st, tr_all.at[pl.ds(4 * theta, 4)], tr_s.at[step], tr_r.at[step],
            (axial, lax.rem(theta + step, 4)),
        )

    chip_backward()

    @pl.when(jnp.logical_and(is_home, y == 3))
    def _():
        home_backward()

    finish_forward()

    @pl.when(jnp.logical_and(is_home, y < 3))
    def _():
        home_backward()

    @pl.when(core == 1)
    def _():
        for line in range(LINES):
            wait_solution(line)
            solve_first(line)
            to_core(line)[1].start()
        for line in range(LINES):
            solve_last(line)

    @pl.when(core == 0)
    def _():
        for line in range(LINES):
            wait_solution(line)
            solve_last(line)

    for step in range(1, 4):
        to_theta(step).start()
    tr_all[pl.ds(4 * theta, 4)] = tr_st[...]

    @pl.when(core == 0)
    def _():
        for line in range(LINES):
            solve_first(line)

    for step in range(1, 4):
        to_theta(step).wait_recv()

    for face in range(LINES):
        total = jnp.zeros((V, FACE), F32)
        for k in range(2):
            source = lax.rem(list_ref[k, face] + angle_ref[0], 16)
            total += apply(split(proj_ref[index_ref[k, face]]), tr_all[source])
        mortar_ref[face] = total

    for i in range(2):
        mine = jnp.logical_and(x == 2 * core + i, core == 1)
        for kind in range(5):
            to_pair(kind, i).wait_send()
            if kind != 3:
                @pl.when(jnp.logical_not(mine))
                def _():
                    to_home(kind, i, x).wait_send()

    @pl.when(is_home)
    def _():
        for way in range(2):
            for chip in range(4):
                mine = jnp.logical_and(x == chip, core == way)

                @pl.when(jnp.logical_not(mine))
                def _():
                    scatter(way, chip).wait_send()

        for chip in range(4):
            @pl.when(jnp.logical_and(x > 1, x != chip))
            def _():
                to_chip(chip).wait_send()

        @pl.when(y < 3)
        def _():
            hop(0).wait_send()

        @pl.when(y > 0)
        def _():
            hop(1).wait_send()

    for line in range(LINES):
        @pl.when(core == 0)
        def _():
            to_core(line)[0].wait_send()

        @pl.when(core == 1)
        def _():
            to_core(line)[1].wait_send()

    for step in range(1, 4):
        to_theta(step).wait_send()


def local(rhs, diag, lower, upper, proj, intersections, index, angle):
    def mats(*lead, kind=F32):
        return pltpu.VMEM((*lead, B, B), kind)

    def vecs(*lead):
        return pltpu.VMEM((*lead, V, B), F32)

    def packs(*lead):
        return pltpu.VMEM((*lead, 800, 128), F32)

    def sems(*shape):
        return pltpu.SemaphoreType.DMA(shape)

    anywhere = pl.BlockSpec(memory_space=pl.ANY)
    vmem = pl.BlockSpec(memory_space=pltpu.VMEM)
    smem = pl.BlockSpec(memory_space=pltpu.SMEM)
    result, mortar = pl.pallas_call(
        kernel,
        out_shape=(
            jax.ShapeDtypeStruct((LINES, 2, V, B), F32),
            jax.ShapeDtypeStruct((LINES, V, FACE), F32),
        ),
        in_specs=[anywhere] * 4 + [vmem] + [smem] * 3,
        out_specs=(vmem, vmem),
        scratch_shapes=[
            mats(4, 2), mats(4, 2), mats(4, 2), vecs(4, 2),
            mats(4, 2, 2, kind=BF16), mats(4, 2, 2, kind=BF16), mats(4, 2, kind=BF16), mats(4, 2, kind=BF16),
            mats(4), mats(4), mats(4), vecs(4, 2), vecs(4), vecs(4),
            mats(2), mats(2), mats(2), vecs(2), vecs(2),
            packs(2), packs(2), mats(2, 2, kind=BF16), vecs(2), vecs(2),
            packs(4), packs(4), vecs(4), vecs(4), mats(4, 2, kind=BF16), vecs(2),
            vecs(), vecs(), vecs(4), vecs(4), vecs(2),
            vecs(4), vecs(4), vecs(4), vecs(4), vecs(4),
            pltpu.VMEM((4, V, FACE), F32), pltpu.VMEM((16, V, FACE), F32),
            sems(4, 4), sems(5, 2), sems(5, 2), sems(5, 2), sems(5, 4), sems(2), sems(2),
            sems(2, 4), sems(4), sems(4), sems(4), sems(4), sems(4), sems(4), sems(2),
        ],
        compiler_params=pltpu.CompilerParams(
            collective_id=0, has_side_effects=True, vmem_limit_bytes=60 * 2**20
        ),
        cost_estimate=pl.CostEstimate(flops=10**10, bytes_accessed=10**7, transcendentals=0),
    )(rhs, diag, lower, upper, proj, intersections.T, index.T, angle)
    return result, mortar.reshape(1, LINES, V * FACE)


def solution(mesh):
    line = P("theta", "axial", None, None)
    return jax.shard_map(
        local,
        mesh=mesh,
        in_specs=(line, line, line, line, P(), P("theta", None), P("theta", None), P()),
        out_specs=(line, P("axial", "theta", None)),
        check_vma=False,
    )
```

```python
import jax
import jax.numpy as jnp
from jax import lax
from jax.experimental import pallas as pl
from jax.experimental.pallas import tpu as pltpu
from jax.sharding import PartitionSpec as P

MESH = pl.DeviceIdType.MESH
F32 = jnp.float32
BF16 = jnp.bfloat16
B = 320
V = 32
FACE = 80
LINES = 4


def split(value):
    high = value.astype(BF16)
    return high, (value - high.astype(F32)).astype(BF16)


def dot(a, b):
    return lax.dot_general(a, b, (((1,), (0,)), ((), ())), preferred_element_type=F32)


def dot_nt(a, b):
    return lax.dot_general(a, b, (((1,), (1,)), ((), ())), preferred_element_type=F32)


def product(a, b):
    left = jnp.concatenate([a[0][:, 256:], a[1][:, 256:], a[0][:, 256:]], 1)
    right = jnp.concatenate([b[0][256:], b[0][256:], b[1][256:]], 0)
    high = a[0][:, :256]
    main = dot(high, b[0][:256]) + dot(a[1][:, :256], b[0][:256]) + dot(high, b[1][:256])
    return main + dot(left, right)


def apply(matrix, vectors):
    high, low = split(vectors)
    both = dot_nt(jnp.concatenate([high, low], 0), matrix[0])
    rows = vectors.shape[0]
    return both[:rows] + both[rows:] + dot_nt(high, matrix[1])


def apply_turned(matrix, vectors):
    high, low = split(vectors)
    both = dot(jnp.concatenate([high, low], 0), matrix[0])
    rows = vectors.shape[0]
    return both[:rows] + both[rows:] + dot(high, matrix[1])


def packed(value):
    rest = value[:, 256:]
    return jnp.concatenate(
        [value[:, :128], value[:, 128:256], jnp.concatenate([rest[:160], rest[160:]], 1)], 0
    )


def unpacked(value):
    rest = value[640:]
    return jnp.concatenate(
        [value[:320], value[320:640], jnp.concatenate([rest[:, :64], rest[:, 64:]], 0)], 1
    )


def kernel(
    rhs_hbm, diag_hbm, lower_hbm, upper_hbm, proj_hbm, list_hbm, index_hbm, angle_hbm,
    out_ref, mortar_ref,
    diag, lower, upper, rhs,
    a_hl, g_hl, t_hl, w_hl, t_f, w_f, e_f, b_v, c_v, d_v,
    t_p, w_p, e_p, c_p, d_p,
    t_c, w_c, e_hl, c_c, d_c,
    t_g, w_g, c_g, d_g, turned, s_chip,
    s_hop, x_hop, s_st, x_st, hop_st,
    s_in, x_in, s_0, s_1, u_0, u_b, w_x, wb_hl,
    tr_st, tr_all, proj_ref, list_ref, index_ref, angle_ref,
    load_sem, table_sem, pair_s, pair_r, home_s, home_r, hop_s, hop_r,
    scat_s, sin_r, xin_r, core_s, tr_s, tr_r, chip_s, chip_r, near_s, u_r, wx_s, wx_r,
):
    axial = lax.axis_index("axial")
    theta = lax.axis_index("theta")
    core = lax.rem(axial, 2)
    x = lax.rem(axial // 2, 4)
    y = axial // 8
    other = 1 - core

    def at(row, chip, which):
        return ((row * 4 + chip) * 2 + which, theta)

    def remote(src, dst, send, recv, device):
        return pltpu.make_async_remote_copy(
            src_ref=src, dst_ref=dst, send_sem=send, recv_sem=recv,
            device_id=device, device_id_type=MESH,
        )

    barrier = pltpu.get_barrier_semaphore()

    def greet(device):
        pl.semaphore_signal(barrier, inc=1, device_id=device, device_id_type=MESH)

    for step in range(1, 8):
        greet((y * 8 + lax.rem(axial + step, 8), theta))
    greet((lax.rem(axial + 8, 32), theta))
    greet((lax.rem(axial + 24, 32), theta))
    for step in range(1, 4):
        greet((axial, lax.rem(theta + step, 4)))

    def load(which, line):
        src, dst = ((diag_hbm, diag), (lower_hbm, lower), (upper_hbm, upper), (rhs_hbm, rhs))[which]
        return pltpu.make_async_copy(src.at[line], dst.at[line], load_sem.at[which, line])

    order = [2 * other, 2 * other + 1, 2 * core, 2 * core + 1]
    for line in order:
        load(0, line).start()
        load(1, line).start()
    for line in order:
        load(3, line).start()
    for line in order:
        load(2, line).start()
    tables = [
        pltpu.make_async_copy(src, dst, table_sem.at[i])
        for i, (src, dst) in enumerate(
            ((proj_hbm, proj_ref), (list_hbm, list_ref), (index_hbm, index_ref), (angle_hbm, angle_ref))
        )
    ]
    for table in tables:
        table.start()

    def whole(ref, *where):
        return ref[(*where, 0)], ref[(*where, 1)]

    def keep(ref, pair, *where):
        ref[(*where, 0)] = pair[0]
        ref[(*where, 1)] = pair[1]

    def first_maps(line):
        load(0, line).wait()
        load(1, line).wait()
        for e in range(2):
            inverse = split(diag[line, e])
            keep(a_hl, split(product(inverse, split(lower[line, e]))), line, e)
        across = product(whole(a_hl, line, 1), whole(a_hl, line, 0))
        t_f[line] = across
        keep(t_hl, split(across), line)

    def first_vectors(line):
        load(3, line).wait()
        for e in range(2):
            b_v[line, e] = apply(split(diag[line, e]), rhs[line, e])
        c_v[line] = b_v[line, 1] - apply(whole(a_hl, line, 1), b_v[line, 0])

    def second_maps(line):
        load(2, line).wait()
        for e in range(2):
            keep(g_hl, split(product(split(diag[line, e]), split(upper[line, e]))), line, e)
        across = product(whole(g_hl, line, 0), whole(g_hl, line, 1))
        w_f[line] = across
        keep(w_hl, split(across), line)

    def third_maps(line):
        first = whole(g_hl, line, 0)
        e_f[line] = -(
            a_hl[line, 0, 0].astype(F32) + a_hl[line, 0, 1].astype(F32)
        ) - product(first, whole(t_hl, line))
        d_v[line] = b_v[line, 0] - apply(first, c_v[line])

    def to_pair(kind, i):
        line = 2 * other + i
        src, dst = ((t_f, t_p), (c_v, c_p), (w_f, w_p), (e_f, e_p), (d_v, d_p))[kind]
        return remote(
            src.at[line], dst.at[i], pair_s.at[kind, i], pair_r.at[kind, i], at(y, x, other)
        )

    gathered = ((t_c, t_g), (c_c, c_g), (w_c, w_g), None, (d_c, d_g))

    def to_home(kind, i, slot):
        src, dst = gathered[kind]
        return remote(
            src.at[i], dst.at[slot], home_s.at[kind, i], home_r.at[kind, slot],
            at(y, 2 * core + i, 1),
        )

    def send_home(kinds, i):
        mine = jnp.logical_and(x == 2 * core + i, core == 1)

        @pl.when(jnp.logical_not(mine))
        def _():
            for kind in kinds:
                to_home(kind, i, x).start()

        @pl.when(mine)
        def _():
            for kind in kinds:
                src, dst = gathered[kind]
                dst[x] = src[i]

    def pair_first(i, carry):
        first_maps(2 * other + i)
        return carry

    def own_first(i, carry):
        first_maps(2 * core + i)
        return carry

    lax.fori_loop(0, 2, pair_first, 0)
    pl.semaphore_wait(barrier, 12)
    for i in range(2):
        to_pair(0, i).start()
    lax.fori_loop(0, 2, own_first, 0)

    def pick(own, given):
        mine = core == 0
        return jnp.where(mine, own, given), jnp.where(mine, given, own)

    def chip_first(i, carry):
        to_pair(0, i).wait_recv()
        t_a, t_b = pick(t_f[2 * core + i], t_p[i])
        t_c[i] = packed(product(split(t_b), split(t_a)))
        send_home((0,), i)
        return carry

    lax.fori_loop(0, 2, chip_first, 0)

    def pair_vectors(i, carry):
        first_vectors(2 * other + i)
        to_pair(1, i).start()
        return carry

    lax.fori_loop(0, 2, pair_vectors, 0)

    def own_vectors(i, carry):
        line = 2 * core + i
        first_vectors(line)
        to_pair(1, i).wait_recv()
        _, t_b = pick(t_f[line], t_p[i])
        c_a, c_b = pick(c_v[line], c_p[i])
        c_c[i] = c_b + apply(split(t_b), c_a)
        send_home((1,), i)
        return carry

    lax.fori_loop(0, 2, own_vectors, 0)

    is_home = core == 1
    zero = jnp.zeros((V, B), F32)

    def arrived(kinds, slot):
        @pl.when(jnp.logical_not(jnp.logical_and(x == slot, x // 2 == 1)))
        def _():
            for kind in kinds:
                to_home(kind, 0, slot).wait_recv()

    def hop(way):
        src, dst, row = ((hop_st.at[0], s_hop, y + 1), (hop_st.at[1], x_hop, y - 1))[way]
        return remote(src, dst, hop_s.at[way], hop_r.at[way], at(row, x, core))

    def scatter(way, chip):
        src, dst, sem = ((s_st, s_in, sin_r), (x_st, x_in, xin_r))[way]
        return remote(src.at[chip], dst.at[x], scat_s.at[way, chip], sem.at[x], at(y, chip, way))

    def scatter_near(chip):
        return remote(x_st.at[chip], x_in.at[x], near_s.at[chip], xin_r.at[x], at(y, chip, 0))

    def to_first(i):
        return remote(w_f.at[2 + i], w_x.at[i], wx_s.at[i], wx_r.at[i], at(y, x, other))

    def to_chip(chip):
        return remote(
            s_st.at[chip], s_chip.at[jnp.maximum(x - 2, 0)], chip_s.at[chip],
            chip_r.at[jnp.maximum(x - 2, 0)], at(y, chip, 1),
        )

    def spread(way):
        for chip in range(4):
            src, dst = ((s_st, s_in), (x_st, x_in))[way]
            mine = jnp.logical_and(x == chip, core == way)

            @pl.when(jnp.logical_not(mine))
            def _():
                scatter(way, chip).start()

            @pl.when(mine)
            def _():
                dst[x] = src[chip]

    def home_forward():
        for chip in range(4):
            arrived((0, 1), chip)
            keep(turned, split(unpacked(t_g[chip]).T), chip)

        @pl.when(y == 0)
        def _():
            s_hop[...] = zero

        @pl.when(y > 0)
        def _():
            hop(0).wait_recv()

        state = s_hop[...]
        for chip in range(4):
            s_st[chip] = state
            state = c_g[chip] + apply_turned(whole(turned, chip), state)
        hop_st[0] = state

        @pl.when(y < 3)
        def _():
            hop(0).start()

        spread(0)
        for chip in range(4):
            @pl.when(jnp.logical_and(x > 1, x != chip))
            def _():
                to_chip(chip).start()

            @pl.when(jnp.logical_and(x > 1, x == chip))
            def _():
                s_chip[x - 2] = s_st[chip]

    def home_backward():
        for chip in (3, 2, 1, 0):
            arrived((2,), chip)
            keep(turned, split(unpacked(w_g[chip]).T), chip)
        for chip in (3, 2, 1, 0):
            arrived((4,), chip)

        @pl.when(y == 3)
        def _():
            x_hop[...] = zero

        @pl.when(y < 3)
        def _():
            hop(1).wait_recv()

        state = x_hop[...]
        for chip in (3, 2, 1, 0):
            x_st[chip] = state
            state = d_g[chip] + apply_turned(whole(turned, chip), state)
        hop_st[1] = state

        @pl.when(y > 0)
        def _():
            hop(1).start()

        for chip in range(4):
            scatter_near(chip).start()
        spread(1)

    def home_at(row, here):
        @pl.when(jnp.logical_and(is_home, jnp.logical_and(y == row, here)))
        def _():
            home_forward()

    def pair_second(i, carry):
        second_maps(2 * other + i)
        to_pair(2, i).start()
        return carry

    lax.fori_loop(0, 2, pair_second, 0)

    def own_second(i, carry):
        home_at(0, i == 1)
        line = 2 * core + i
        second_maps(line)
        to_pair(2, i).wait_recv()
        w_a, w_b = pick(w_f[line], w_p[i])
        w_c[i] = packed(product(split(w_a), split(w_b)))
        send_home((2,), i)
        return carry

    lax.fori_loop(0, 2, own_second, 0)

    @pl.when(core == 1)
    def _():
        for i in range(2):
            to_first(i).start()


    def pair_third(i, carry):
        home_at(1, i == 0)
        third_maps(2 * other + i)
        to_pair(3, i).start()
        to_pair(4, i).start()
        return carry

    lax.fori_loop(0, 2, pair_third, 0)

    def own_third(i, carry):
        home_at(2, i == 1)
        line = 2 * core + i
        third_maps(line)
        to_pair(3, i).wait_recv()
        to_pair(4, i).wait_recv()
        t_a, _ = pick(t_f[line], t_p[i])
        c_a, _ = pick(c_v[line], c_p[i])
        w_a, _ = pick(w_f[line], w_p[i])
        e_a, e_b = pick(e_f[line], e_p[i])
        d_a, d_b = pick(d_v[line], d_p[i])
        w_a = split(w_a)
        e_b = split(e_b)
        keep(e_hl, split(e_a + product(w_a, split(product(e_b, split(t_a))))), i)
        d_c[i] = d_a + apply(w_a, d_b + apply(e_b, c_a))
        return carry

    lax.fori_loop(0, 2, own_third, 0)
    home_at(3, True)

    def to_core(line):
        forward = remote(
            s_1.at[line], s_in.at[line], core_s.at[line], sin_r.at[line], at(y, x, other)
        )
        back = remote(
            u_0.at[line], u_b.at[line], core_s.at[line], u_r.at[line], at(y, x, other)
        )
        return forward, back

    def chip_backward():
        for i in range(2):
            @pl.when(core == 0)
            def _():
                to_core(i)[0].wait_recv()
                d_c[i] = d_c[i] + apply(whole(e_hl, i), s_in[i])

            @pl.when(core == 1)
            def _():
                @pl.when(x != 2 + i)
                def _():
                    remote(
                        s_st.at[0], s_chip.at[i], chip_s.at[0], chip_r.at[i], at(y, x, other)
                    ).wait_recv()

                d_c[i] = d_c[i] + apply(whole(e_hl, i), s_chip[i])

            send_home((4,), i)

    def wait_solution(line):
        mine = jnp.logical_and(is_home, jnp.logical_and(x == line, core == 1))

        @pl.when(jnp.logical_not(mine))
        def _():
            remote(
                x_st.at[0], x_in.at[line], near_s.at[0], xin_r.at[line], at(y, x, other)
            ).wait_recv()

    def finish_forward():
        for line in range(LINES):
            @pl.when(jnp.logical_or(core == 1, line > 1))
            def _():
                to_core(line)[0].wait_recv()

            s_1[line] = c_v[line] + apply(whole(t_hl, line), s_in[line])

            @pl.when(core == 0)
            def _():
                to_core(line)[0].start()

        for line in range(LINES):
            s_0[line] = b_v[line, 0] - apply(whole(a_hl, line, 0), s_in[line])
            u_0[line] = s_0[line] - apply(whole(g_hl, line, 0), s_1[line])

            @pl.when(core == 1)
            def _():
                to_core(line)[1].start()

        @pl.when(core == 0)
        def _():
            for i in range(2):
                keep(wb_hl, split(w_p[i]), i)
                to_first(i).wait_recv()
                keep(wb_hl, split(w_x[i]), 2 + i)
            for line in range(LINES):
                to_core(line)[1].wait_recv()

    def solve_first(line):
        out_ref[line, 0] = u_0[line] + apply(whole(w_hl, line), x_in[line])

    def solve_last(line):
        value = s_1[line] - apply(whole(g_hl, line, 1), x_in[line])
        out_ref[line, 1] = value
        tr_st[line] = value[:, B - FACE :]

    def to_theta(step):
        return remote(
            tr_st, tr_all.at[pl.ds(4 * theta, 4)], tr_s.at[step], tr_r.at[step],
            (axial, lax.rem(theta + step, 4)),
        )

    chip_backward()

    @pl.when(jnp.logical_and(is_home, y == 3))
    def _():
        home_backward()

    finish_forward()

    @pl.when(jnp.logical_and(is_home, y < 3))
    def _():
        home_backward()

    @pl.when(core == 1)
    def _():
        for line in range(LINES):
            wait_solution(line)
            solve_last(line)

    @pl.when(core == 0)
    def _():
        for line in range(LINES):
            wait_solution(line)
            x_in[line] = u_b[line] + apply(whole(wb_hl, line), x_in[line])
        for line in range(LINES):
            solve_last(line)

    for step in range(1, 4):
        to_theta(step).start()
    tr_all[pl.ds(4 * theta, 4)] = tr_st[...]

    for line in range(LINES):
        solve_first(line)

    for step in range(1, 4):
        to_theta(step).wait_recv()

    for table in tables:
        table.wait()
    for face in range(LINES):
        total = jnp.zeros((V, FACE), F32)
        for k in range(2):
            source = lax.rem(list_ref[k, face] + angle_ref[0], 16)
            total += apply(split(proj_ref[index_ref[k, face]]), tr_all[source])
        mortar_ref[face] = total

    for i in range(2):
        mine = jnp.logical_and(x == 2 * core + i, core == 1)
        for kind in range(5):
            to_pair(kind, i).wait_send()
            if kind != 3:
                @pl.when(jnp.logical_not(mine))
                def _():
                    to_home(kind, i, x).wait_send()

    @pl.when(is_home)
    def _():
        for way in range(2):
            for chip in range(4):
                mine = jnp.logical_and(x == chip, core == way)

                @pl.when(jnp.logical_not(mine))
                def _():
                    scatter(way, chip).wait_send()

        for i in range(2):
            to_first(i).wait_send()
        for chip in range(4):
            scatter_near(chip).wait_send()

            @pl.when(jnp.logical_and(x > 1, x != chip))
            def _():
                to_chip(chip).wait_send()

        @pl.when(y < 3)
        def _():
            hop(0).wait_send()

        @pl.when(y > 0)
        def _():
            hop(1).wait_send()

    for line in range(LINES):
        @pl.when(core == 0)
        def _():
            to_core(line)[0].wait_send()

        @pl.when(core == 1)
        def _():
            to_core(line)[1].wait_send()

    for step in range(1, 4):
        to_theta(step).wait_send()


def local(rhs, diag, lower, upper, proj, intersections, index, angle):
    def mats(*lead, kind=F32):
        return pltpu.VMEM((*lead, B, B), kind)

    def vecs(*lead):
        return pltpu.VMEM((*lead, V, B), F32)

    def packs(*lead):
        return pltpu.VMEM((*lead, 800, 128), F32)

    def sems(*shape):
        return pltpu.SemaphoreType.DMA(shape)

    anywhere = pl.BlockSpec(memory_space=pl.ANY)
    vmem = pl.BlockSpec(memory_space=pltpu.VMEM)
    result, mortar = pl.pallas_call(
        kernel,
        out_shape=(
            jax.ShapeDtypeStruct((LINES, 2, V, B), F32),
            jax.ShapeDtypeStruct((LINES, V, FACE), F32),
        ),
        in_specs=[anywhere] * 8,
        out_specs=(vmem, vmem),
        scratch_shapes=[
            mats(4, 2), mats(4, 2), mats(4, 2), vecs(4, 2),
            mats(4, 2, 2, kind=BF16), mats(4, 2, 2, kind=BF16), mats(4, 2, kind=BF16), mats(4, 2, kind=BF16),
            mats(4), mats(4), mats(4), vecs(4, 2), vecs(4), vecs(4),
            mats(2), mats(2), mats(2), vecs(2), vecs(2),
            packs(2), packs(2), mats(2, 2, kind=BF16), vecs(2), vecs(2),
            packs(4), packs(4), vecs(4), vecs(4), mats(4, 2, kind=BF16), vecs(2),
            vecs(), vecs(), vecs(4), vecs(4), vecs(2),
            vecs(4), vecs(4), vecs(4), vecs(4), vecs(4), vecs(4), mats(2), mats(4, 2, kind=BF16),
            pltpu.VMEM((4, V, FACE), F32), pltpu.VMEM((16, V, FACE), F32),
            pltpu.VMEM((16, FACE, FACE), F32), pltpu.SMEM((2, 4), jnp.int32), pltpu.SMEM((2, 4), jnp.int32),
            pltpu.SMEM((1,), jnp.int32),
            sems(4, 4), sems(4), sems(5, 2), sems(5, 2), sems(5, 2), sems(5, 4), sems(2), sems(2),
            sems(2, 4), sems(4), sems(4), sems(4), sems(4), sems(4), sems(4), sems(2), sems(4), sems(4), sems(2), sems(2),
        ],
        compiler_params=pltpu.CompilerParams(
            collective_id=0, has_side_effects=True, vmem_limit_bytes=60 * 2**20
        ),
        cost_estimate=pl.CostEstimate(flops=10**10, bytes_accessed=10**7, transcendentals=0),
    )(rhs, diag, lower, upper, proj, intersections.T, index.T, angle)
    return result, mortar.reshape(1, LINES, V * FACE)


def solution(mesh):
    line = P("theta", "axial", None, None)
    return jax.shard_map(
        local,
        mesh=mesh,
        in_specs=(line, line, line, line, P(), P("theta", None), P("theta", None), P()),
        out_specs=(line, P("axial", "theta", None)),
        check_vma=False,
    )
```

```python
import jax
import jax.numpy as jnp
from jax import lax
from jax.experimental import pallas as pl
from jax.experimental.pallas import tpu as pltpu
from jax.sharding import PartitionSpec as P

MESH = pl.DeviceIdType.MESH
F32 = jnp.float32
BF16 = jnp.bfloat16
B = 320
V = 32
FACE = 80
LINES = 4


def split(value):
    high = value.astype(BF16)
    return high, (value - high.astype(F32)).astype(BF16)


def dot(a, b):
    return lax.dot_general(a, b, (((1,), (0,)), ((), ())), preferred_element_type=F32)


def dot_nt(a, b):
    return lax.dot_general(a, b, (((1,), (1,)), ((), ())), preferred_element_type=F32)


def product(a, b):
    left = jnp.concatenate([a[0][:, 256:], a[1][:, 256:], a[0][:, 256:]], 1)
    right = jnp.concatenate([b[0][256:], b[0][256:], b[1][256:]], 0)
    high = a[0][:, :256]
    main = dot(high, b[0][:256]) + dot(a[1][:, :256], b[0][:256]) + dot(high, b[1][:256])
    return main + dot(left, right)


def apply(matrix, vectors):
    high, low = split(vectors)
    both = dot_nt(jnp.concatenate([high, low], 0), matrix[0])
    rows = vectors.shape[0]
    return both[:rows] + both[rows:] + dot_nt(high, matrix[1])


def apply_turned(matrix, vectors):
    high, low = split(vectors)
    rows = vectors.shape[0]
    both = jnp.concatenate([high, low], 0)
    none = jnp.zeros((rows, 64), BF16)
    left = jnp.concatenate([both[:, 256:], jnp.concatenate([high[:, 256:], none], 0)], 1)
    right = jnp.concatenate([matrix[0][256:], matrix[1][256:]], 0)
    main = dot(both[:, :256], matrix[0][:256]) + dot(left, right)
    return main[:rows] + main[rows:] + dot(high[:, :256], matrix[1][:256])


def packed(value):
    rest = value[:, 256:]
    return jnp.concatenate(
        [value[:, :128], value[:, 128:256], jnp.concatenate([rest[:160], rest[160:]], 1)], 0
    )


def unpacked(value):
    rest = value[640:]
    return jnp.concatenate(
        [value[:320], value[320:640], jnp.concatenate([rest[:, :64], rest[:, 64:]], 0)], 1
    )


def kernel(
    rhs_hbm, diag_hbm, lower_hbm, upper_hbm, proj_hbm, list_hbm, index_hbm, angle_hbm,
    out_ref, mortar_ref,
    diag, lower, upper, rhs,
    a_hl, g_hl, t_hl, w_hl, t_f, w_f, e_f, b_v, c_v, d_v,
    t_p, w_p, e_p, c_p, d_p,
    t_c, w_c, e_hl, c_c, d_c,
    t_g, w_g, c_g, d_g, turned, s_chip,
    s_hop, x_hop, s_st, x_st, hop_st,
    s_in, x_in, s_0, s_1, u_0, u_b, w_x, wb_hl,
    tr_st, tr_all, proj_ref, list_ref, index_ref, angle_ref,
    load_sem, table_sem, pair_s, pair_r, home_s, home_r, hop_s, hop_r,
    scat_s, sin_r, xin_r, core_s, tr_s, tr_r, chip_s, chip_r, near_s, u_r, wx_s, wx_r,
):
    axial = lax.axis_index("axial")
    theta = lax.axis_index("theta")
    core = lax.rem(axial, 2)
    x = lax.rem(axial // 2, 4)
    y = axial // 8
    other = 1 - core

    def at(row, chip, which):
        return ((row * 4 + chip) * 2 + which, theta)

    def remote(src, dst, send, recv, device):
        return pltpu.make_async_remote_copy(
            src_ref=src, dst_ref=dst, send_sem=send, recv_sem=recv,
            device_id=device, device_id_type=MESH,
        )

    barrier = pltpu.get_barrier_semaphore()

    def greet(device):
        pl.semaphore_signal(barrier, inc=1, device_id=device, device_id_type=MESH)

    for step in range(1, 8):
        greet((y * 8 + lax.rem(axial + step, 8), theta))
    greet((lax.rem(axial + 8, 32), theta))
    greet((lax.rem(axial + 24, 32), theta))
    for step in range(1, 4):
        greet((axial, lax.rem(theta + step, 4)))

    def load(which, line):
        src, dst = ((diag_hbm, diag), (lower_hbm, lower), (upper_hbm, upper), (rhs_hbm, rhs))[which]
        return pltpu.make_async_copy(src.at[line], dst.at[line], load_sem.at[which, line])

    order = [2 * other, 2 * other + 1, 2 * core, 2 * core + 1]
    for line in order:
        load(0, line).start()
        load(1, line).start()
    for line in order:
        load(3, line).start()
    for line in order:
        load(2, line).start()
    tables = [
        pltpu.make_async_copy(src, dst, table_sem.at[i])
        for i, (src, dst) in enumerate(
            ((proj_hbm, proj_ref), (list_hbm, list_ref), (index_hbm, index_ref), (angle_hbm, angle_ref))
        )
    ]
    for table in tables:
        table.start()

    def whole(ref, *where):
        return ref[(*where, 0)], ref[(*where, 1)]

    def keep(ref, pair, *where):
        ref[(*where, 0)] = pair[0]
        ref[(*where, 1)] = pair[1]

    def first_maps(line):
        load(0, line).wait()
        load(1, line).wait()
        for e in range(2):
            inverse = split(diag[line, e])
            keep(a_hl, split(product(inverse, split(lower[line, e]))), line, e)
        across = product(whole(a_hl, line, 1), whole(a_hl, line, 0))
        t_f[line] = across
        keep(t_hl, split(across), line)

    def first_vectors(line):
        load(3, line).wait()
        for e in range(2):
            b_v[line, e] = apply(split(diag[line, e]), rhs[line, e])
        c_v[line] = b_v[line, 1] - apply(whole(a_hl, line, 1), b_v[line, 0])

    def second_maps(line):
        load(2, line).wait()
        for e in range(2):
            keep(g_hl, split(product(split(diag[line, e]), split(upper[line, e]))), line, e)
        across = product(whole(g_hl, line, 0), whole(g_hl, line, 1))
        w_f[line] = across
        keep(w_hl, split(across), line)

    def third_maps(line):
        first = whole(g_hl, line, 0)
        e_f[line] = -(
            a_hl[line, 0, 0].astype(F32) + a_hl[line, 0, 1].astype(F32)
        ) - product(first, whole(t_hl, line))
        d_v[line] = b_v[line, 0] - apply(first, c_v[line])

    def to_pair(kind, i):
        line = 2 * other + i
        src, dst = ((t_f, t_p), (c_v, c_p), (w_f, w_p), (e_f, e_p), (d_v, d_p))[kind]
        return remote(
            src.at[line], dst.at[i], pair_s.at[kind, i], pair_r.at[kind, i], at(y, x, other)
        )

    gathered = ((t_c, t_g), (c_c, c_g), (w_c, w_g), None, (d_c, d_g))

    def to_home(kind, i, slot):
        src, dst = gathered[kind]
        return remote(
            src.at[i], dst.at[slot], home_s.at[kind, i], home_r.at[kind, slot],
            at(y, 2 * core + i, 1),
        )

    def send_home(kinds, i):
        mine = jnp.logical_and(x == 2 * core + i, core == 1)

        @pl.when(jnp.logical_not(mine))
        def _():
            for kind in kinds:
                to_home(kind, i, x).start()

        @pl.when(mine)
        def _():
            for kind in kinds:
                src, dst = gathered[kind]
                dst[x] = src[i]

    def pair_first(i, carry):
        first_maps(2 * other + i)
        return carry

    def own_first(i, carry):
        first_maps(2 * core + i)
        return carry

    lax.fori_loop(0, 2, pair_first, 0)
    pl.semaphore_wait(barrier, 12)
    for i in range(2):
        to_pair(0, i).start()
    lax.fori_loop(0, 2, own_first, 0)

    def pick(own, given):
        mine = core == 0
        return jnp.where(mine, own, given), jnp.where(mine, given, own)

    def chip_first(i, carry):
        to_pair(0, i).wait_recv()
        t_a, t_b = pick(t_f[2 * core + i], t_p[i])
        t_c[i] = packed(product(split(t_b), split(t_a)))
        send_home((0,), i)
        return carry

    lax.fori_loop(0, 2, chip_first, 0)

    def pair_vectors(i, carry):
        first_vectors(2 * other + i)
        to_pair(1, i).start()
        return carry

    lax.fori_loop(0, 2, pair_vectors, 0)

    def own_vectors(i, carry):
        line = 2 * core + i
        first_vectors(line)
        to_pair(1, i).wait_recv()
        _, t_b = pick(t_f[line], t_p[i])
        c_a, c_b = pick(c_v[line], c_p[i])
        c_c[i] = c_b + apply(split(t_b), c_a)
        send_home((1,), i)
        return carry

    lax.fori_loop(0, 2, own_vectors, 0)

    is_home = core == 1
    zero = jnp.zeros((V, B), F32)

    def arrived(kinds, slot):
        @pl.when(jnp.logical_not(jnp.logical_and(x == slot, x // 2 == 1)))
        def _():
            for kind in kinds:
                to_home(kind, 0, slot).wait_recv()

    def hop(way):
        src, dst, row = ((hop_st.at[0], s_hop, y + 1), (hop_st.at[1], x_hop, y - 1))[way]
        return remote(src, dst, hop_s.at[way], hop_r.at[way], at(row, x, core))

    def scatter(way, chip):
        src, dst, sem = ((s_st, s_in, sin_r), (x_st, x_in, xin_r))[way]
        return remote(src.at[chip], dst.at[x], scat_s.at[way, chip], sem.at[x], at(y, chip, way))

    def scatter_near(chip):
        return remote(x_st.at[chip], x_in.at[x], near_s.at[chip], xin_r.at[x], at(y, chip, 0))

    def to_first(i):
        return remote(w_f.at[2 + i], w_x.at[i], wx_s.at[i], wx_r.at[i], at(y, x, other))

    def to_chip(chip):
        return remote(
            s_st.at[chip], s_chip.at[jnp.maximum(x - 2, 0)], chip_s.at[chip],
            chip_r.at[jnp.maximum(x - 2, 0)], at(y, chip, 1),
        )

    def spread(way):
        for chip in range(4):
            src, dst = ((s_st, s_in), (x_st, x_in))[way]
            mine = jnp.logical_and(x == chip, core == way)

            @pl.when(jnp.logical_not(mine))
            def _():
                scatter(way, chip).start()

            @pl.when(mine)
            def _():
                dst[x] = src[chip]

    def home_forward():
        for chip in range(4):
            arrived((0, 1), chip)
            keep(turned, split(unpacked(t_g[chip]).T), chip)

        @pl.when(y == 0)
        def _():
            s_hop[...] = zero

        @pl.when(y > 0)
        def _():
            hop(0).wait_recv()

        state = s_hop[...]
        for chip in range(4):
            s_st[chip] = state
            state = c_g[chip] + apply_turned(whole(turned, chip), state)
        hop_st[0] = state

        @pl.when(y < 3)
        def _():
            hop(0).start()

        spread(0)
        for chip in range(4):
            @pl.when(jnp.logical_and(x > 1, x != chip))
            def _():
                to_chip(chip).start()

            @pl.when(jnp.logical_and(x > 1, x == chip))
            def _():
                s_chip[x - 2] = s_st[chip]

    def home_backward():
        for chip in (3, 2, 1, 0):
            arrived((2,), chip)
            keep(turned, split(unpacked(w_g[chip]).T), chip)
        for chip in (3, 2, 1, 0):
            arrived((4,), chip)

        @pl.when(y == 3)
        def _():
            x_hop[...] = zero

        @pl.when(y < 3)
        def _():
            hop(1).wait_recv()

        state = x_hop[...]
        for chip in (3, 2, 1, 0):
            x_st[chip] = state
            state = d_g[chip] + apply_turned(whole(turned, chip), state)
        hop_st[1] = state

        @pl.when(y > 0)
        def _():
            hop(1).start()

        for chip in range(4):
            scatter_near(chip).start()
        spread(1)

    def home_at(row, here):
        @pl.when(jnp.logical_and(is_home, jnp.logical_and(y == row, here)))
        def _():
            home_forward()

    def pair_second(i, carry):
        second_maps(2 * other + i)
        to_pair(2, i).start()
        return carry

    lax.fori_loop(0, 2, pair_second, 0)

    def own_second(i, carry):
        home_at(0, i == 1)
        line = 2 * core + i
        second_maps(line)
        to_pair(2, i).wait_recv()
        w_a, w_b = pick(w_f[line], w_p[i])
        w_c[i] = packed(product(split(w_a), split(w_b)))
        send_home((2,), i)
        return carry

    lax.fori_loop(0, 2, own_second, 0)

    @pl.when(core == 1)
    def _():
        for i in range(2):
            to_first(i).start()


    def pair_third(i, carry):
        home_at(1, i == 0)
        third_maps(2 * other + i)
        to_pair(3, i).start()
        to_pair(4, i).start()
        return carry

    lax.fori_loop(0, 2, pair_third, 0)

    def own_third(i, carry):
        home_at(2, i == 1)
        line = 2 * core + i
        third_maps(line)
        to_pair(3, i).wait_recv()
        to_pair(4, i).wait_recv()
        t_a, _ = pick(t_f[line], t_p[i])
        c_a, _ = pick(c_v[line], c_p[i])
        w_a, _ = pick(w_f[line], w_p[i])
        e_a, e_b = pick(e_f[line], e_p[i])
        d_a, d_b = pick(d_v[line], d_p[i])
        w_a = split(w_a)
        e_b = split(e_b)
        keep(e_hl, split(e_a + product(w_a, split(product(e_b, split(t_a))))), i)
        d_c[i] = d_a + apply(w_a, d_b + apply(e_b, c_a))
        return carry

    lax.fori_loop(0, 2, own_third, 0)
    home_at(3, True)

    def to_core(line):
        forward = remote(
            s_1.at[line], s_in.at[line], core_s.at[line], sin_r.at[line], at(y, x, other)
        )
        back = remote(
            u_0.at[line], u_b.at[line], core_s.at[line], u_r.at[line], at(y, x, other)
        )
        return forward, back

    def chip_backward():
        for i in range(2):
            @pl.when(core == 0)
            def _():
                to_core(i)[0].wait_recv()
                d_c[i] = d_c[i] + apply(whole(e_hl, i), s_in[i])

            @pl.when(core == 1)
            def _():
                @pl.when(x != 2 + i)
                def _():
                    remote(
                        s_st.at[0], s_chip.at[i], chip_s.at[0], chip_r.at[i], at(y, x, other)
                    ).wait_recv()

                d_c[i] = d_c[i] + apply(whole(e_hl, i), s_chip[i])

            send_home((4,), i)

    def wait_solution(line):
        mine = jnp.logical_and(is_home, jnp.logical_and(x == line, core == 1))

        @pl.when(jnp.logical_not(mine))
        def _():
            remote(
                x_st.at[0], x_in.at[line], near_s.at[0], xin_r.at[line], at(y, x, other)
            ).wait_recv()

    def finish_forward():
        for line in range(LINES):
            @pl.when(jnp.logical_or(core == 1, line > 1))
            def _():
                to_core(line)[0].wait_recv()

            s_1[line] = c_v[line] + apply(whole(t_hl, line), s_in[line])

            @pl.when(core == 0)
            def _():
                to_core(line)[0].start()

        for line in range(LINES):
            s_0[line] = b_v[line, 0] - apply(whole(a_hl, line, 0), s_in[line])
            u_0[line] = s_0[line] - apply(whole(g_hl, line, 0), s_1[line])

            @pl.when(core == 1)
            def _():
                to_core(line)[1].start()

        @pl.when(core == 0)
        def _():
            for i in range(2):
                keep(wb_hl, split(w_p[i]), i)
                to_first(i).wait_recv()
                keep(wb_hl, split(w_x[i]), 2 + i)
            for line in range(LINES):
                to_core(line)[1].wait_recv()

    def solve_first(line):
        out_ref[line, 0] = u_0[line] + apply(whole(w_hl, line), x_in[line])

    def solve_last(line):
        value = s_1[line] - apply(whole(g_hl, line, 1), x_in[line])
        out_ref[line, 1] = value

    def trace(line):
        face = g_hl[line, 1, 0, B - FACE :, :], g_hl[line, 1, 1, B - FACE :, :]
        tr_st[line] = s_1[line][:, B - FACE :] - apply(face, x_in[line])

    def to_theta(step):
        return remote(
            tr_st, tr_all.at[pl.ds(4 * theta, 4)], tr_s.at[step], tr_r.at[step],
            (axial, lax.rem(theta + step, 4)),
        )

    chip_backward()

    @pl.when(jnp.logical_and(is_home, y == 3))
    def _():
        home_backward()

    finish_forward()

    @pl.when(jnp.logical_and(is_home, y < 3))
    def _():
        home_backward()

    @pl.when(core == 1)
    def _():
        for line in range(LINES):
            wait_solution(line)
            trace(line)

    @pl.when(core == 0)
    def _():
        for line in range(LINES):
            wait_solution(line)
            x_in[line] = u_b[line] + apply(whole(wb_hl, line), x_in[line])
        for line in range(LINES):
            trace(line)

    for step in range(1, 4):
        to_theta(step).start()
    tr_all[pl.ds(4 * theta, 4)] = tr_st[...]

    for line in range(LINES):
        solve_last(line)
        solve_first(line)

    for step in range(1, 4):
        to_theta(step).wait_recv()

    for table in tables:
        table.wait()
    for face in range(LINES):
        total = jnp.zeros((V, FACE), F32)
        for k in range(2):
            source = lax.rem(list_ref[k, face] + angle_ref[0], 16)
            total += apply(split(proj_ref[index_ref[k, face]]), tr_all[source])
        mortar_ref[face] = total

    for i in range(2):
        mine = jnp.logical_and(x == 2 * core + i, core == 1)
        for kind in range(5):
            to_pair(kind, i).wait_send()
            if kind != 3:
                @pl.when(jnp.logical_not(mine))
                def _():
                    to_home(kind, i, x).wait_send()

    @pl.when(is_home)
    def _():
        for way in range(2):
            for chip in range(4):
                mine = jnp.logical_and(x == chip, core == way)

                @pl.when(jnp.logical_not(mine))
                def _():
                    scatter(way, chip).wait_send()

        for i in range(2):
            to_first(i).wait_send()
        for chip in range(4):
            scatter_near(chip).wait_send()

            @pl.when(jnp.logical_and(x > 1, x != chip))
            def _():
                to_chip(chip).wait_send()

        @pl.when(y < 3)
        def _():
            hop(0).wait_send()

        @pl.when(y > 0)
        def _():
            hop(1).wait_send()

    for line in range(LINES):
        @pl.when(core == 0)
        def _():
            to_core(line)[0].wait_send()

        @pl.when(core == 1)
        def _():
            to_core(line)[1].wait_send()

    for step in range(1, 4):
        to_theta(step).wait_send()


def local(rhs, diag, lower, upper, proj, intersections, index, angle):
    def mats(*lead, kind=F32):
        return pltpu.VMEM((*lead, B, B), kind)

    def vecs(*lead):
        return pltpu.VMEM((*lead, V, B), F32)

    def packs(*lead):
        return pltpu.VMEM((*lead, 800, 128), F32)

    def sems(*shape):
        return pltpu.SemaphoreType.DMA(shape)

    anywhere = pl.BlockSpec(memory_space=pl.ANY)
    vmem = pl.BlockSpec(memory_space=pltpu.VMEM)
    result, mortar = pl.pallas_call(
        kernel,
        out_shape=(
            jax.ShapeDtypeStruct((LINES, 2, V, B), F32),
            jax.ShapeDtypeStruct((LINES, V, FACE), F32),
        ),
        in_specs=[anywhere] * 8,
        out_specs=(vmem, vmem),
        scratch_shapes=[
            mats(4, 2), mats(4, 2), mats(4, 2), vecs(4, 2),
            mats(4, 2, 2, kind=BF16), mats(4, 2, 2, kind=BF16), mats(4, 2, kind=BF16), mats(4, 2, kind=BF16),
            mats(4), mats(4), mats(4), vecs(4, 2), vecs(4), vecs(4),
            mats(2), mats(2), mats(2), vecs(2), vecs(2),
            packs(2), packs(2), mats(2, 2, kind=BF16), vecs(2), vecs(2),
            packs(4), packs(4), vecs(4), vecs(4), mats(4, 2, kind=BF16), vecs(2),
            vecs(), vecs(), vecs(4), vecs(4), vecs(2),
            vecs(4), vecs(4), vecs(4), vecs(4), vecs(4), vecs(4), mats(2), mats(4, 2, kind=BF16),
            pltpu.VMEM((4, V, FACE), F32), pltpu.VMEM((16, V, FACE), F32),
            pltpu.VMEM((16, FACE, FACE), F32), pltpu.SMEM((2, 4), jnp.int32), pltpu.SMEM((2, 4), jnp.int32),
            pltpu.SMEM((1,), jnp.int32),
            sems(4, 4), sems(4), sems(5, 2), sems(5, 2), sems(5, 2), sems(5, 4), sems(2), sems(2),
            sems(2, 4), sems(4), sems(4), sems(4), sems(4), sems(4), sems(4), sems(2), sems(4), sems(4), sems(2), sems(2),
        ],
        compiler_params=pltpu.CompilerParams(
            collective_id=0, has_side_effects=True, vmem_limit_bytes=60 * 2**20
        ),
        cost_estimate=pl.CostEstimate(flops=10**10, bytes_accessed=10**7, transcendentals=0),
    )(rhs, diag, lower, upper, proj, intersections.T, index.T, angle)
    return result, mortar.reshape(1, LINES, V * FACE)


def solution(mesh):
    line = P("theta", "axial", None, None)
    return jax.shard_map(
        local,
        mesh=mesh,
        in_specs=(line, line, line, line, P(), P("theta", None), P("theta", None), P()),
        out_specs=(line, P("axial", "theta", None)),
        check_vma=False,
    )
```

```python
import jax
import jax.numpy as jnp
from jax import lax
from jax.experimental import pallas as pl
from jax.experimental.pallas import tpu as pltpu
from jax.sharding import PartitionSpec as P

MESH = pl.DeviceIdType.MESH
F32 = jnp.float32
BF16 = jnp.bfloat16
B = 320
V = 32
FACE = 80
LINES = 4


def split(value):
    high = value.astype(BF16)
    return high, (value - high.astype(F32)).astype(BF16)


def dot(a, b):
    return lax.dot_general(a, b, (((1,), (0,)), ((), ())), preferred_element_type=F32)


def dot_nt(a, b):
    return lax.dot_general(a, b, (((1,), (1,)), ((), ())), preferred_element_type=F32)


def product(a, b):
    left = jnp.concatenate([a[0][:, 256:], a[1][:, 256:], a[0][:, 256:]], 1)
    right = jnp.concatenate([b[0][256:], b[0][256:], b[1][256:]], 0)
    high = a[0][:, :256]
    main = dot(high, b[0][:256]) + dot(a[1][:, :256], b[0][:256]) + dot(high, b[1][:256])
    return main + dot(left, right)


def apply(matrix, vectors):
    high, low = split(vectors)
    both = dot_nt(jnp.concatenate([high, low], 0), matrix[0])
    rows = vectors.shape[0]
    return both[:rows] + both[rows:] + dot_nt(high, matrix[1])


def apply_turned(matrix, vectors):
    high, low = split(vectors)
    both = dot(jnp.concatenate([high, low], 0), matrix[0])
    rows = vectors.shape[0]
    return both[:rows] + both[rows:] + dot(high, matrix[1])


def packed(value):
    rest = value[:, 256:]
    return jnp.concatenate(
        [value[:, :128], value[:, 128:256], jnp.concatenate([rest[:160], rest[160:]], 1)], 0
    )


def unpacked(value):
    rest = value[640:]
    return jnp.concatenate(
        [value[:320], value[320:640], jnp.concatenate([rest[:, :64], rest[:, 64:]], 0)], 1
    )


def kernel(
    rhs_hbm, diag_hbm, lower_hbm, upper_hbm, proj_hbm, list_hbm, index_hbm, angle_hbm,
    out_ref, mortar_ref,
    diag, lower, upper, rhs,
    a_hl, g_hl, t_hl, w_hl, t_f, w_f, e_f, b_v, c_v, d_v,
    t_p, w_p, e_p, c_p, d_p,
    t_c, w_c, e_hl, c_c, d_c,
    t_g, w_g, c_g, d_g, turned, s_chip,
    s_hop, x_hop, s_st, x_st, hop_st,
    s_in, x_in, s_0, s_1, u_0, u_b, w_x, wb_hl,
    tr_st, tr_all, proj_ref, list_ref, index_ref, angle_ref,
    load_sem, table_sem, pair_s, pair_r, home_s, home_r, hop_s, hop_r,
    scat_s, sin_r, xin_r, core_s, tr_s, tr_r, chip_s, chip_r, near_s, u_r, wx_s, wx_r,
):
    axial = lax.axis_index("axial")
    theta = lax.axis_index("theta")
    core = lax.rem(axial, 2)
    x = lax.rem(axial // 2, 4)
    y = axial // 8
    other = 1 - core

    def at(row, chip, which):
        return ((row * 4 + chip) * 2 + which, theta)

    def remote(src, dst, send, recv, device):
        return pltpu.make_async_remote_copy(
            src_ref=src, dst_ref=dst, send_sem=send, recv_sem=recv,
            device_id=device, device_id_type=MESH,
        )

    barrier = pltpu.get_barrier_semaphore()

    def greet(device):
        pl.semaphore_signal(barrier, inc=1, device_id=device, device_id_type=MESH)

    for step in range(1, 8):
        greet((y * 8 + lax.rem(axial + step, 8), theta))
    greet((lax.rem(axial + 8, 32), theta))
    greet((lax.rem(axial + 24, 32), theta))
    for step in range(1, 4):
        greet((axial, lax.rem(theta + step, 4)))

    def load(which, line):
        src, dst = ((diag_hbm, diag), (lower_hbm, lower), (upper_hbm, upper), (rhs_hbm, rhs))[which]
        return pltpu.make_async_copy(src.at[line], dst.at[line], load_sem.at[which, line])

    order = [2 * other, 2 * other + 1, 2 * core, 2 * core + 1]
    for line in order:
        load(0, line).start()
        load(1, line).start()
    for line in order:
        load(3, line).start()
    for line in order:
        load(2, line).start()
    tables = [
        pltpu.make_async_copy(src, dst, table_sem.at[i])
        for i, (src, dst) in enumerate(
            ((proj_hbm, proj_ref), (list_hbm, list_ref), (index_hbm, index_ref), (angle_hbm, angle_ref))
        )
    ]
    for table in tables:
        table.start()

    def whole(ref, *where):
        return ref[(*where, 0)], ref[(*where, 1)]

    def keep(ref, pair, *where):
        ref[(*where, 0)] = pair[0]
        ref[(*where, 1)] = pair[1]

    def first_maps(line):
        load(0, line).wait()
        load(1, line).wait()
        for e in range(2):
            inverse = split(diag[line, e])
            keep(a_hl, split(product(inverse, split(lower[line, e]))), line, e)
        across = product(whole(a_hl, line, 1), whole(a_hl, line, 0))
        t_f[line] = across
        keep(t_hl, split(across), line)

    def first_vectors(line):
        load(3, line).wait()
        for e in range(2):
            b_v[line, e] = apply(split(diag[line, e]), rhs[line, e])
        c_v[line] = b_v[line, 1] - apply(whole(a_hl, line, 1), b_v[line, 0])

    def second_maps(line):
        load(2, line).wait()
        for e in range(2):
            keep(g_hl, split(product(split(diag[line, e]), split(upper[line, e]))), line, e)
        across = product(whole(g_hl, line, 0), whole(g_hl, line, 1))
        w_f[line] = across
        keep(w_hl, split(across), line)

    def third_maps(line):
        first = whole(g_hl, line, 0)
        e_f[line] = -(
            a_hl[line, 0, 0].astype(F32) + a_hl[line, 0, 1].astype(F32)
        ) - product(first, whole(t_hl, line))
        d_v[line] = b_v[line, 0] - apply(first, c_v[line])

    def to_pair(kind, i):
        line = 2 * other + i
        src, dst = ((t_f, t_p), (c_v, c_p), (w_f, w_p), (e_f, e_p), (d_v, d_p))[kind]
        return remote(
            src.at[line], dst.at[i], pair_s.at[kind, i], pair_r.at[kind, i], at(y, x, other)
        )

    gathered = ((t_c, t_g), (c_c, c_g), (w_c, w_g), None, (d_c, d_g))

    def to_home(kind, i, slot):
        src, dst = gathered[kind]
        return remote(
            src.at[i], dst.at[slot], home_s.at[kind, i], home_r.at[kind, slot],
            at(y, 2 * core + i, 1),
        )

    def send_home(kinds, i):
        mine = jnp.logical_and(x == 2 * core + i, core == 1)

        @pl.when(jnp.logical_not(mine))
        def _():
            for kind in kinds:
                to_home(kind, i, x).start()

        @pl.when(mine)
        def _():
            for kind in kinds:
                src, dst = gathered[kind]
                dst[x] = src[i]

    def pair_first(i, carry):
        first_maps(2 * other + i)
        return carry

    def own_first(i, carry):
        first_maps(2 * core + i)
        return carry

    lax.fori_loop(0, 2, pair_first, 0)
    pl.semaphore_wait(barrier, 12)
    for i in range(2):
        to_pair(0, i).start()
    lax.fori_loop(0, 2, own_first, 0)

    def pick(own, given):
        mine = core == 0
        return jnp.where(mine, own, given), jnp.where(mine, given, own)

    def chip_first(i, carry):
        to_pair(0, i).wait_recv()
        t_a, t_b = pick(t_f[2 * core + i], t_p[i])
        t_c[i] = packed(product(split(t_b), split(t_a)))
        send_home((0,), i)
        return carry

    lax.fori_loop(0, 2, chip_first, 0)

    def pair_vectors(i, carry):
        first_vectors(2 * other + i)
        to_pair(1, i).start()
        return carry

    lax.fori_loop(0, 2, pair_vectors, 0)

    def own_vectors(i, carry):
        line = 2 * core + i
        first_vectors(line)
        to_pair(1, i).wait_recv()
        _, t_b = pick(t_f[line], t_p[i])
        c_a, c_b = pick(c_v[line], c_p[i])
        c_c[i] = c_b + apply(split(t_b), c_a)
        send_home((1,), i)
        return carry

    lax.fori_loop(0, 2, own_vectors, 0)

    is_home = core == 1
    zero = jnp.zeros((V, B), F32)

    def arrived(kinds, slot):
        @pl.when(jnp.logical_not(jnp.logical_and(x == slot, x // 2 == 1)))
        def _():
            for kind in kinds:
                to_home(kind, 0, slot).wait_recv()

    def hop(way):
        src, dst, row = ((hop_st.at[0], s_hop, y + 1), (hop_st.at[1], x_hop, y - 1))[way]
        return remote(src, dst, hop_s.at[way], hop_r.at[way], at(row, x, core))

    def scatter(way, chip):
        src, dst, sem = ((s_st, s_in, sin_r), (x_st, x_in, xin_r))[way]
        return remote(src.at[chip], dst.at[x], scat_s.at[way, chip], sem.at[x], at(y, chip, way))

    def scatter_near(chip):
        return remote(x_st.at[chip], x_in.at[x], near_s.at[chip], xin_r.at[x], at(y, chip, 0))

    def to_first(i):
        return remote(w_f.at[2 + i], w_x.at[i], wx_s.at[i], wx_r.at[i], at(y, x, other))

    def to_chip(chip):
        return remote(
            s_st.at[chip], s_chip.at[jnp.maximum(x - 2, 0)], chip_s.at[chip],
            chip_r.at[jnp.maximum(x - 2, 0)], at(y, chip, 1),
        )

    def send_state(chip):
        @pl.when(jnp.logical_and(x > 1, x != chip))
        def _():
            to_chip(chip).start()

        @pl.when(jnp.logical_and(x > 1, x == chip))
        def _():
            s_chip[x - 2] = s_st[chip]

        scatter(0, chip).start()

    def send_solution(chip):
        scatter_near(chip).start()

        @pl.when(x != chip)
        def _():
            scatter(1, chip).start()

        @pl.when(x == chip)
        def _():
            x_in[x] = x_st[chip]

    def home_forward():
        for chip in range(4):
            arrived((0, 1), chip)
            keep(turned, split(unpacked(t_g[chip]).T), chip)

        @pl.when(y == 0)
        def _():
            s_hop[...] = zero

        @pl.when(y > 0)
        def _():
            hop(0).wait_recv()

        state = s_hop[...]
        for chip in range(4):
            s_st[chip] = state

            @pl.when(y == 3)
            def _():
                send_state(chip)

            state = c_g[chip] + apply_turned(whole(turned, chip), state)
        hop_st[0] = state

        @pl.when(y < 3)
        def _():
            hop(0).start()
            for chip in range(4):
                send_state(chip)

    def home_backward():
        for chip in (3, 2, 1, 0):
            arrived((2,), chip)
            keep(turned, split(unpacked(w_g[chip]).T), chip)
        for chip in (3, 2, 1, 0):
            arrived((4,), chip)

        @pl.when(y == 3)
        def _():
            x_hop[...] = zero

        @pl.when(y < 3)
        def _():
            hop(1).wait_recv()

        state = x_hop[...]
        for chip in (3, 2, 1, 0):
            x_st[chip] = state

            @pl.when(y == 0)
            def _():
                send_solution(chip)

            state = d_g[chip] + apply_turned(whole(turned, chip), state)
        hop_st[1] = state

        @pl.when(y > 0)
        def _():
            hop(1).start()
            for chip in (3, 2, 1, 0):
                send_solution(chip)

    def home_at(row, here):
        @pl.when(jnp.logical_and(is_home, jnp.logical_and(y == row, here)))
        def _():
            home_forward()

    def pair_second(i, carry):
        second_maps(2 * other + i)
        to_pair(2, i).start()
        return carry

    lax.fori_loop(0, 2, pair_second, 0)

    def own_second(i, carry):
        home_at(0, i == 1)
        line = 2 * core + i
        second_maps(line)
        to_pair(2, i).wait_recv()
        w_a, w_b = pick(w_f[line], w_p[i])
        w_c[i] = packed(product(split(w_a), split(w_b)))
        send_home((2,), i)
        return carry

    lax.fori_loop(0, 2, own_second, 0)

    @pl.when(core == 1)
    def _():
        for i in range(2):
            to_first(i).start()


    def pair_third(i, carry):
        home_at(1, i == 0)
        third_maps(2 * other + i)
        to_pair(3, i).start()
        to_pair(4, i).start()
        return carry

    lax.fori_loop(0, 2, pair_third, 0)

    def own_third(i, carry):
        home_at(2, i == 1)
        line = 2 * core + i
        third_maps(line)
        to_pair(3, i).wait_recv()
        to_pair(4, i).wait_recv()
        t_a, _ = pick(t_f[line], t_p[i])
        c_a, _ = pick(c_v[line], c_p[i])
        w_a, _ = pick(w_f[line], w_p[i])
        e_a, e_b = pick(e_f[line], e_p[i])
        d_a, d_b = pick(d_v[line], d_p[i])
        w_a = split(w_a)
        e_b = split(e_b)
        keep(e_hl, split(e_a + product(w_a, split(product(e_b, split(t_a))))), i)
        d_c[i] = d_a + apply(w_a, d_b + apply(e_b, c_a))
        return carry

    lax.fori_loop(0, 2, own_third, 0)
    home_at(3, True)

    def to_core(line):
        forward = remote(
            s_1.at[line], s_in.at[line], core_s.at[line], sin_r.at[line], at(y, x, other)
        )
        back = remote(
            u_0.at[line], u_b.at[line], core_s.at[line], u_r.at[line], at(y, x, other)
        )
        return forward, back

    def chip_backward():
        for i in range(2):
            @pl.when(core == 0)
            def _():
                to_core(i)[0].wait_recv()
                d_c[i] = d_c[i] + apply(whole(e_hl, i), s_in[i])

            @pl.when(core == 1)
            def _():
                @pl.when(x != 2 + i)
                def _():
                    remote(
                        s_st.at[0], s_chip.at[i], chip_s.at[0], chip_r.at[i], at(y, x, other)
                    ).wait_recv()

                d_c[i] = d_c[i] + apply(whole(e_hl, i), s_chip[i])

            send_home((4,), i)

    def wait_solution(line):
        mine = jnp.logical_and(is_home, jnp.logical_and(x == line, core == 1))

        @pl.when(jnp.logical_not(mine))
        def _():
            remote(
                x_st.at[0], x_in.at[line], near_s.at[0], xin_r.at[line], at(y, x, other)
            ).wait_recv()

    def finish_forward():
        for line in range(LINES):
            @pl.when(jnp.logical_or(core == 1, line > 1))
            def _():
                to_core(line)[0].wait_recv()

            s_1[line] = c_v[line] + apply(whole(t_hl, line), s_in[line])

            @pl.when(core == 0)
            def _():
                to_core(line)[0].start()

        for line in range(LINES):
            s_0[line] = b_v[line, 0] - apply(whole(a_hl, line, 0), s_in[line])
            u_0[line] = s_0[line] - apply(whole(g_hl, line, 0), s_1[line])

            @pl.when(core == 1)
            def _():
                to_core(line)[1].start()

        @pl.when(core == 0)
        def _():
            for i in range(2):
                keep(wb_hl, split(w_p[i]), i)
                to_first(i).wait_recv()
                keep(wb_hl, split(w_x[i]), 2 + i)
            for line in range(LINES):
                to_core(line)[1].wait_recv()

    def solve_first(line):
        out_ref[line, 0] = u_0[line] + apply(whole(w_hl, line), x_in[line])

    def solve_last(line):
        value = s_1[line] - apply(whole(g_hl, line, 1), x_in[line])
        out_ref[line, 1] = value
        tr_st[line] = value[:, B - FACE :]

    def to_theta(step):
        return remote(
            tr_st, tr_all.at[pl.ds(4 * theta, 4)], tr_s.at[step], tr_r.at[step],
            (axial, lax.rem(theta + step, 4)),
        )

    chip_backward()

    @pl.when(jnp.logical_and(is_home, y == 3))
    def _():
        home_backward()

    finish_forward()

    @pl.when(jnp.logical_and(is_home, y < 3))
    def _():
        home_backward()

    @pl.when(core == 1)
    def _():
        for line in range(LINES):
            wait_solution(line)
            solve_last(line)

    @pl.when(core == 0)
    def _():
        for line in range(LINES):
            wait_solution(line)
            x_in[line] = u_b[line] + apply(whole(wb_hl, line), x_in[line])
        for line in range(LINES):
            solve_last(line)

    for step in range(1, 4):
        to_theta(step).start()
    tr_all[pl.ds(4 * theta, 4)] = tr_st[...]

    for line in range(LINES):
        solve_first(line)

    for step in range(1, 4):
        to_theta(step).wait_recv()

    for table in tables:
        table.wait()
    for face in range(LINES):
        total = jnp.zeros((V, FACE), F32)
        for k in range(2):
            source = lax.rem(list_ref[k, face] + angle_ref[0], 16)
            total += apply(split(proj_ref[index_ref[k, face]]), tr_all[source])
        mortar_ref[face] = total

    for i in range(2):
        mine = jnp.logical_and(x == 2 * core + i, core == 1)
        for kind in range(5):
            to_pair(kind, i).wait_send()
            if kind != 3:
                @pl.when(jnp.logical_not(mine))
                def _():
                    to_home(kind, i, x).wait_send()

    @pl.when(is_home)
    def _():
        for way in range(2):
            for chip in range(4):
                mine = jnp.logical_and(x == chip, core == way)

                @pl.when(jnp.logical_not(mine))
                def _():
                    scatter(way, chip).wait_send()

        for i in range(2):
            to_first(i).wait_send()
        for chip in range(4):
            scatter_near(chip).wait_send()

            @pl.when(jnp.logical_and(x > 1, x != chip))
            def _():
                to_chip(chip).wait_send()

        @pl.when(y < 3)
        def _():
            hop(0).wait_send()

        @pl.when(y > 0)
        def _():
            hop(1).wait_send()

    for line in range(LINES):
        @pl.when(core == 0)
        def _():
            to_core(line)[0].wait_send()

        @pl.when(core == 1)
        def _():
            to_core(line)[1].wait_send()

    for step in range(1, 4):
        to_theta(step).wait_send()


def local(rhs, diag, lower, upper, proj, intersections, index, angle):
    def mats(*lead, kind=F32):
        return pltpu.VMEM((*lead, B, B), kind)

    def vecs(*lead):
        return pltpu.VMEM((*lead, V, B), F32)

    def packs(*lead):
        return pltpu.VMEM((*lead, 800, 128), F32)

    def sems(*shape):
        return pltpu.SemaphoreType.DMA(shape)

    anywhere = pl.BlockSpec(memory_space=pl.ANY)
    vmem = pl.BlockSpec(memory_space=pltpu.VMEM)
    result, mortar = pl.pallas_call(
        kernel,
        out_shape=(
            jax.ShapeDtypeStruct((LINES, 2, V, B), F32),
            jax.ShapeDtypeStruct((LINES, V, FACE), F32),
        ),
        in_specs=[anywhere] * 8,
        out_specs=(vmem, vmem),
        scratch_shapes=[
            mats(4, 2), mats(4, 2), mats(4, 2), vecs(4, 2),
            mats(4, 2, 2, kind=BF16), mats(4, 2, 2, kind=BF16), mats(4, 2, kind=BF16), mats(4, 2, kind=BF16),
            mats(4), mats(4), mats(4), vecs(4, 2), vecs(4), vecs(4),
            mats(2), mats(2), mats(2), vecs(2), vecs(2),
            packs(2), packs(2), mats(2, 2, kind=BF16), vecs(2), vecs(2),
            packs(4), packs(4), vecs(4), vecs(4), mats(4, 2, kind=BF16), vecs(2),
            vecs(), vecs(), vecs(4), vecs(4), vecs(2),
            vecs(4), vecs(4), vecs(4), vecs(4), vecs(4), vecs(4), mats(2), mats(4, 2, kind=BF16),
            pltpu.VMEM((4, V, FACE), F32), pltpu.VMEM((16, V, FACE), F32),
            pltpu.VMEM((16, FACE, FACE), F32), pltpu.SMEM((2, 4), jnp.int32), pltpu.SMEM((2, 4), jnp.int32),
            pltpu.SMEM((1,), jnp.int32),
            sems(4, 4), sems(4), sems(5, 2), sems(5, 2), sems(5, 2), sems(5, 4), sems(2), sems(2),
            sems(2, 4), sems(4), sems(4), sems(4), sems(4), sems(4), sems(4), sems(2), sems(4), sems(4), sems(2), sems(2),
        ],
        compiler_params=pltpu.CompilerParams(
            collective_id=0, has_side_effects=True, vmem_limit_bytes=60 * 2**20
        ),
        cost_estimate=pl.CostEstimate(flops=10**10, bytes_accessed=10**7, transcendentals=0),
    )(rhs, diag, lower, upper, proj, intersections.T, index.T, angle)
    return result, mortar.reshape(1, LINES, V * FACE)


def solution(mesh):
    line = P("theta", "axial", None, None)
    return jax.shard_map(
        local,
        mesh=mesh,
        in_specs=(line, line, line, line, P(), P("theta", None), P("theta", None), P()),
        out_specs=(line, P("axial", "theta", None)),
        check_vma=False,
    )
```

```python
import jax
import jax.numpy as jnp
from jax import lax
from jax.experimental import pallas as pl
from jax.experimental.pallas import tpu as pltpu
from jax.sharding import PartitionSpec as P

MESH = pl.DeviceIdType.MESH
F32 = jnp.float32
BF16 = jnp.bfloat16
B = 320
V = 32
FACE = 80
LINES = 4


def split(value):
    high = value.astype(BF16)
    return high, (value - high.astype(F32)).astype(BF16)


def dot(a, b):
    return lax.dot_general(a, b, (((1,), (0,)), ((), ())), preferred_element_type=F32)


def dot_nt(a, b):
    return lax.dot_general(a, b, (((1,), (1,)), ((), ())), preferred_element_type=F32)


def product(a, b):
    left = jnp.concatenate([a[0][:, 256:], a[1][:, 256:], a[0][:, 256:]], 1)
    right = jnp.concatenate([b[0][256:], b[0][256:], b[1][256:]], 0)
    high = a[0][:, :256]
    main = dot(high, b[0][:256]) + dot(a[1][:, :256], b[0][:256]) + dot(high, b[1][:256])
    return main + dot(left, right)


def apply(matrix, vectors):
    high, low = split(vectors)
    both = dot_nt(jnp.concatenate([high, low], 0), matrix[0])
    rows = vectors.shape[0]
    return both[:rows] + both[rows:] + dot_nt(high, matrix[1])


def apply_turned(matrix, vectors):
    high, low = split(vectors)
    both = dot(jnp.concatenate([high, low], 0), matrix[0])
    rows = vectors.shape[0]
    return both[:rows] + both[rows:] + dot(high, matrix[1])


def packed(value):
    rest = value[:, 256:]
    return jnp.concatenate(
        [value[:, :128], value[:, 128:256], jnp.concatenate([rest[:160], rest[160:]], 1)], 0
    )


def unpacked(value):
    rest = value[640:]
    return jnp.concatenate(
        [value[:320], value[320:640], jnp.concatenate([rest[:, :64], rest[:, 64:]], 0)], 1
    )


def kernel(
    rhs_hbm, diag_hbm, lower_hbm, upper_hbm, proj_hbm, list_hbm, index_hbm, angle_hbm,
    out_ref, mortar_ref,
    diag, lower, upper, rhs,
    a_hl, g_hl, t_hl, w_hl, t_f, w_f, e_f, b_v, c_v, d_v,
    t_p, w_p, e_p, c_p, d_p,
    t_c, w_c, e_hl, c_c, d_c,
    t_g, w_g, c_g, d_g, turned, s_chip,
    s_hop, x_hop, s_st, x_st, hop_st,
    s_in, x_in, s_0, s_1, u_0, u_b, w_x, wb_hl,
    tr_st, tr_all, proj_ref, list_ref, index_ref, angle_ref,
    load_sem, table_sem, pair_s, pair_r, home_s, home_r, hop_s, hop_r,
    scat_s, sin_r, xin_r, core_s, tr_s, tr_r, chip_s, chip_r, near_s, u_r, wx_s, wx_r,
):
    axial = lax.axis_index("axial")
    theta = lax.axis_index("theta")
    core = lax.rem(axial, 2)
    x = lax.rem(axial // 2, 4)
    y = axial // 8
    other = 1 - core

    def at(row, chip, which):
        return ((row * 4 + chip) * 2 + which, theta)

    def remote(src, dst, send, recv, device):
        return pltpu.make_async_remote_copy(
            src_ref=src, dst_ref=dst, send_sem=send, recv_sem=recv,
            device_id=device, device_id_type=MESH,
        )

    barrier = pltpu.get_barrier_semaphore()

    def greet(device):
        pl.semaphore_signal(barrier, inc=1, device_id=device, device_id_type=MESH)

    for step in range(1, 8):
        greet((y * 8 + lax.rem(axial + step, 8), theta))
    greet((lax.rem(axial + 8, 32), theta))
    greet((lax.rem(axial + 24, 32), theta))
    for step in range(1, 4):
        greet((axial, lax.rem(theta + step, 4)))

    def load(which, line):
        src, dst = ((diag_hbm, diag), (lower_hbm, lower), (upper_hbm, upper), (rhs_hbm, rhs))[which]
        return pltpu.make_async_copy(src.at[line], dst.at[line], load_sem.at[which, line])

    order = [2 * other, 2 * other + 1, 2 * core, 2 * core + 1]
    for line in order:
        load(0, line).start()
        load(1, line).start()
    for line in order:
        load(3, line).start()
    for line in order:
        load(2, line).start()
    tables = [
        pltpu.make_async_copy(src, dst, table_sem.at[i])
        for i, (src, dst) in enumerate(
            ((proj_hbm, proj_ref), (list_hbm, list_ref), (index_hbm, index_ref), (angle_hbm, angle_ref))
        )
    ]
    for table in tables:
        table.start()

    def whole(ref, *where):
        return ref[(*where, 0)], ref[(*where, 1)]

    def keep(ref, pair, *where):
        ref[(*where, 0)] = pair[0]
        ref[(*where, 1)] = pair[1]

    def first_maps(line):
        load(0, line).wait()
        load(1, line).wait()
        for e in range(2):
            inverse = split(diag[line, e])
            keep(a_hl, split(product(inverse, split(lower[line, e]))), line, e)
        across = product(whole(a_hl, line, 1), whole(a_hl, line, 0))
        t_f[line] = across
        keep(t_hl, split(across), line)

    def first_vectors(line):
        load(3, line).wait()
        for e in range(2):
            b_v[line, e] = apply(split(diag[line, e]), rhs[line, e])
        c_v[line] = b_v[line, 1] - apply(whole(a_hl, line, 1), b_v[line, 0])

    def second_maps(line):
        load(2, line).wait()
        for e in range(2):
            keep(g_hl, split(product(split(diag[line, e]), split(upper[line, e]))), line, e)
        across = product(whole(g_hl, line, 0), whole(g_hl, line, 1))
        w_f[line] = across
        keep(w_hl, split(across), line)

    def third_maps(line):
        first = whole(g_hl, line, 0)
        e_f[line] = -(
            a_hl[line, 0, 0].astype(F32) + a_hl[line, 0, 1].astype(F32)
        ) - product(first, whole(t_hl, line))
        d_v[line] = b_v[line, 0] - apply(first, c_v[line])

    def to_pair(kind, i):
        line = 2 * other + i
        src, dst = ((t_f, t_p), (c_v, c_p), (w_f, w_p), (e_f, e_p), (d_v, d_p))[kind]
        return remote(
            src.at[line], dst.at[i], pair_s.at[kind, i], pair_r.at[kind, i], at(y, x, other)
        )

    gathered = ((t_c, t_g), (c_c, c_g), (w_c, w_g), None, (d_c, d_g))

    def to_home(kind, i, slot):
        src, dst = gathered[kind]
        return remote(
            src.at[i], dst.at[slot], home_s.at[kind, i], home_r.at[kind, slot],
            at(y, 2 * core + i, 1),
        )

    def send_home(kinds, i):
        mine = jnp.logical_and(x == 2 * core + i, core == 1)

        @pl.when(jnp.logical_not(mine))
        def _():
            for kind in kinds:
                to_home(kind, i, x).start()

        @pl.when(mine)
        def _():
            for kind in kinds:
                src, dst = gathered[kind]
                dst[x] = src[i]

    def pair_first(i, carry):
        first_maps(2 * other + i)
        return carry

    def own_first(i, carry):
        first_maps(2 * core + i)
        return carry

    lax.fori_loop(0, 2, pair_first, 0)
    pl.semaphore_wait(barrier, 12)
    for i in range(2):
        to_pair(0, i).start()
    lax.fori_loop(0, 2, own_first, 0)

    def pick(own, given):
        mine = core == 0
        return jnp.where(mine, own, given), jnp.where(mine, given, own)

    def chip_first(i, carry):
        to_pair(0, i).wait_recv()
        t_a, t_b = pick(t_f[2 * core + i], t_p[i])
        t_c[i] = packed(product(split(t_b), split(t_a)))
        send_home((0,), i)
        return carry

    lax.fori_loop(0, 2, chip_first, 0)

    def pair_vectors(i, carry):
        first_vectors(2 * other + i)
        to_pair(1, i).start()
        return carry

    lax.fori_loop(0, 2, pair_vectors, 0)

    def own_vectors(i, carry):
        line = 2 * core + i
        first_vectors(line)
        to_pair(1, i).wait_recv()
        _, t_b = pick(t_f[line], t_p[i])
        c_a, c_b = pick(c_v[line], c_p[i])
        c_c[i] = c_b + apply(split(t_b), c_a)
        send_home((1,), i)
        return carry

    lax.fori_loop(0, 2, own_vectors, 0)

    is_home = core == 1
    zero = jnp.zeros((V, B), F32)

    def arrived(kinds, slot):
        @pl.when(jnp.logical_not(jnp.logical_and(x == slot, x // 2 == 1)))
        def _():
            for kind in kinds:
                to_home(kind, 0, slot).wait_recv()

    def hop(way):
        src, dst, row = ((hop_st.at[0], s_hop, y + 1), (hop_st.at[1], x_hop, y - 1))[way]
        return remote(src, dst, hop_s.at[way], hop_r.at[way], at(row, x, core))

    def scatter(way, chip):
        src, dst, sem = ((s_st, s_in, sin_r), (x_st, x_in, xin_r))[way]
        return remote(src.at[chip], dst.at[x], scat_s.at[way, chip], sem.at[x], at(y, chip, way))

    def scatter_near(chip):
        return remote(x_st.at[chip], x_in.at[x], near_s.at[chip], xin_r.at[x], at(y, chip, 0))

    def to_first(i):
        return remote(w_f.at[2 + i], w_x.at[i], wx_s.at[i], wx_r.at[i], at(y, x, other))

    def to_chip(chip):
        return remote(
            s_st.at[chip], s_chip.at[jnp.maximum(x - 2, 0)], chip_s.at[chip],
            chip_r.at[jnp.maximum(x - 2, 0)], at(y, chip, 1),
        )

    def send_state(chip):
        @pl.when(jnp.logical_and(x > 1, x != chip))
        def _():
            to_chip(chip).start()

        @pl.when(jnp.logical_and(x > 1, x == chip))
        def _():
            s_chip[x - 2] = s_st[chip]

        scatter(0, chip).start()

    def send_solution(chip):
        scatter_near(chip).start()

        @pl.when(x != chip)
        def _():
            scatter(1, chip).start()

        @pl.when(x == chip)
        def _():
            x_in[x] = x_st[chip]

    def home_forward():
        for chip in range(4):
            arrived((0, 1), chip)
            keep(turned, split(unpacked(t_g[chip]).T), chip)

        @pl.when(y == 0)
        def _():
            s_hop[...] = zero

        @pl.when(y > 0)
        def _():
            hop(0).wait_recv()

        state = s_hop[...]
        for chip in range(4):
            s_st[chip] = state

            @pl.when(y == 3)
            def _():
                send_state(chip)

            state = c_g[chip] + apply_turned(whole(turned, chip), state)
        hop_st[0] = state

        @pl.when(y < 3)
        def _():
            hop(0).start()
            for chip in range(4):
                send_state(chip)

    def home_backward():
        for chip in (3, 2, 1, 0):
            arrived((2,), chip)
            keep(turned, split(unpacked(w_g[chip]).T), chip)
        for chip in (3, 2, 1, 0):
            arrived((4,), chip)

        @pl.when(y == 3)
        def _():
            x_hop[...] = zero

        @pl.when(y < 3)
        def _():
            hop(1).wait_recv()

        state = x_hop[...]
        for chip in (3, 2, 1, 0):
            x_st[chip] = state

            @pl.when(y == 0)
            def _():
                send_solution(chip)

            state = d_g[chip] + apply_turned(whole(turned, chip), state)
        hop_st[1] = state

        @pl.when(y > 0)
        def _():
            hop(1).start()
            for chip in (3, 2, 1, 0):
                send_solution(chip)

    def home_at(row, here):
        @pl.when(jnp.logical_and(is_home, jnp.logical_and(y == row, here)))
        def _():
            home_forward()

    def pair_second(i, carry):
        second_maps(2 * other + i)
        to_pair(2, i).start()
        return carry

    lax.fori_loop(0, 2, pair_second, 0)

    def own_second(i, carry):
        home_at(0, i == 1)
        line = 2 * core + i
        second_maps(line)
        to_pair(2, i).wait_recv()
        w_a, w_b = pick(w_f[line], w_p[i])
        w_c[i] = packed(product(split(w_a), split(w_b)))
        send_home((2,), i)
        return carry

    lax.fori_loop(0, 2, own_second, 0)

    @pl.when(core == 1)
    def _():
        for i in range(2):
            to_first(i).start()


    def pair_third(i, carry):
        home_at(1, i == 0)
        third_maps(2 * other + i)
        to_pair(3, i).start()
        to_pair(4, i).start()
        return carry

    lax.fori_loop(0, 2, pair_third, 0)

    def own_third(i, carry):
        home_at(2, i == 1)
        line = 2 * core + i
        third_maps(line)
        to_pair(3, i).wait_recv()
        to_pair(4, i).wait_recv()
        t_a, _ = pick(t_f[line], t_p[i])
        c_a, _ = pick(c_v[line], c_p[i])
        w_a, _ = pick(w_f[line], w_p[i])
        e_a, e_b = pick(e_f[line], e_p[i])
        d_a, d_b = pick(d_v[line], d_p[i])
        w_a = split(w_a)
        e_b = split(e_b)
        keep(e_hl, split(e_a + product(w_a, split(product(e_b, split(t_a))))), i)
        d_c[i] = d_a + apply(w_a, d_b + apply(e_b, c_a))
        return carry

    lax.fori_loop(0, 2, own_third, 0)
    home_at(3, True)

    def to_core(line):
        forward = remote(
            s_1.at[line], s_in.at[line], core_s.at[line], sin_r.at[line], at(y, x, other)
        )
        back = remote(
            u_0.at[line], u_b.at[line], core_s.at[line], u_r.at[line], at(y, x, other)
        )
        return forward, back

    def chip_backward():
        for i in range(2):
            @pl.when(core == 0)
            def _():
                to_core(i)[0].wait_recv()
                d_c[i] = d_c[i] + apply(whole(e_hl, i), s_in[i])

            @pl.when(core == 1)
            def _():
                @pl.when(x != 2 + i)
                def _():
                    remote(
                        s_st.at[0], s_chip.at[i], chip_s.at[0], chip_r.at[i], at(y, x, other)
                    ).wait_recv()

                d_c[i] = d_c[i] + apply(whole(e_hl, i), s_chip[i])

            send_home((4,), i)

    def wait_solution(line):
        mine = jnp.logical_and(is_home, jnp.logical_and(x == line, core == 1))

        @pl.when(jnp.logical_not(mine))
        def _():
            remote(
                x_st.at[0], x_in.at[line], near_s.at[0], xin_r.at[line], at(y, x, other)
            ).wait_recv()

    def finish_forward():
        for line in range(LINES):
            @pl.when(jnp.logical_or(core == 1, line > 1))
            def _():
                to_core(line)[0].wait_recv()

            s_1[line] = c_v[line] + apply(whole(t_hl, line), s_in[line])

            @pl.when(core == 0)
            def _():
                to_core(line)[0].start()

        for line in range(LINES):
            s_0[line] = b_v[line, 0] - apply(whole(a_hl, line, 0), s_in[line])
            u_0[line] = s_0[line] - apply(whole(g_hl, line, 0), s_1[line])

            @pl.when(core == 1)
            def _():
                to_core(line)[1].start()

        @pl.when(core == 0)
        def _():
            for i in range(2):
                keep(wb_hl, split(w_p[i]), i)
                to_first(i).wait_recv()
                keep(wb_hl, split(w_x[i]), 2 + i)
            for line in range(LINES):
                to_core(line)[1].wait_recv()

    def solve_first(line):
        out_ref[line, 0] = u_0[line] + apply(whole(w_hl, line), x_in[line])

    def solve_last(line):
        value = s_1[line] - apply(whole(g_hl, line, 1), x_in[line])
        out_ref[line, 1] = value

    def trace(line):
        face = g_hl[line, 1, 0, B - FACE :, :], g_hl[line, 1, 1, B - FACE :, :]
        tr_st[line] = s_1[line][:, B - FACE :] - apply(face, x_in[line])

    def to_theta(step):
        return remote(
            tr_st, tr_all.at[pl.ds(4 * theta, 4)], tr_s.at[step], tr_r.at[step],
            (axial, lax.rem(theta + step, 4)),
        )

    chip_backward()

    @pl.when(jnp.logical_and(is_home, y == 3))
    def _():
        home_backward()

    finish_forward()

    @pl.when(jnp.logical_and(is_home, y < 3))
    def _():
        home_backward()

    @pl.when(core == 1)
    def _():
        for line in range(LINES):
            wait_solution(line)
            trace(line)

    @pl.when(core == 0)
    def _():
        for line in range(LINES):
            wait_solution(line)
            x_in[line] = u_b[line] + apply(whole(wb_hl, line), x_in[line])
        for line in range(LINES):
            trace(line)

    for step in range(1, 4):
        to_theta(step).start()
    tr_all[pl.ds(4 * theta, 4)] = tr_st[...]

    for line in range(LINES):
        solve_last(line)
        solve_first(line)

    for step in range(1, 4):
        to_theta(step).wait_recv()

    for table in tables:
        table.wait()
    for face in range(LINES):
        total = jnp.zeros((V, FACE), F32)
        for k in range(2):
            source = lax.rem(list_ref[k, face] + angle_ref[0], 16)
            total += apply(split(proj_ref[index_ref[k, face]]), tr_all[source])
        mortar_ref[face] = total

    for i in range(2):
        mine = jnp.logical_and(x == 2 * core + i, core == 1)
        for kind in range(5):
            to_pair(kind, i).wait_send()
            if kind != 3:
                @pl.when(jnp.logical_not(mine))
                def _():
                    to_home(kind, i, x).wait_send()

    @pl.when(is_home)
    def _():
        for way in range(2):
            for chip in range(4):
                mine = jnp.logical_and(x == chip, core == way)

                @pl.when(jnp.logical_not(mine))
                def _():
                    scatter(way, chip).wait_send()

        for i in range(2):
            to_first(i).wait_send()
        for chip in range(4):
            scatter_near(chip).wait_send()

            @pl.when(jnp.logical_and(x > 1, x != chip))
            def _():
                to_chip(chip).wait_send()

        @pl.when(y < 3)
        def _():
            hop(0).wait_send()

        @pl.when(y > 0)
        def _():
            hop(1).wait_send()

    for line in range(LINES):
        @pl.when(core == 0)
        def _():
            to_core(line)[0].wait_send()

        @pl.when(core == 1)
        def _():
            to_core(line)[1].wait_send()

    for step in range(1, 4):
        to_theta(step).wait_send()


def local(rhs, diag, lower, upper, proj, intersections, index, angle):
    def mats(*lead, kind=F32):
        return pltpu.VMEM((*lead, B, B), kind)

    def vecs(*lead):
        return pltpu.VMEM((*lead, V, B), F32)

    def packs(*lead):
        return pltpu.VMEM((*lead, 800, 128), F32)

    def sems(*shape):
        return pltpu.SemaphoreType.DMA(shape)

    anywhere = pl.BlockSpec(memory_space=pl.ANY)
    vmem = pl.BlockSpec(memory_space=pltpu.VMEM)
    result, mortar = pl.pallas_call(
        kernel,
        out_shape=(
            jax.ShapeDtypeStruct((LINES, 2, V, B), F32),
            jax.ShapeDtypeStruct((LINES, V, FACE), F32),
        ),
        in_specs=[anywhere] * 8,
        out_specs=(vmem, vmem),
        scratch_shapes=[
            mats(4, 2), mats(4, 2), mats(4, 2), vecs(4, 2),
            mats(4, 2, 2, kind=BF16), mats(4, 2, 2, kind=BF16), mats(4, 2, kind=BF16), mats(4, 2, kind=BF16),
            mats(4), mats(4), mats(4), vecs(4, 2), vecs(4), vecs(4),
            mats(2), mats(2), mats(2), vecs(2), vecs(2),
            packs(2), packs(2), mats(2, 2, kind=BF16), vecs(2), vecs(2),
            packs(4), packs(4), vecs(4), vecs(4), mats(4, 2, kind=BF16), vecs(2),
            vecs(), vecs(), vecs(4), vecs(4), vecs(2),
            vecs(4), vecs(4), vecs(4), vecs(4), vecs(4), vecs(4), mats(2), mats(4, 2, kind=BF16),
            pltpu.VMEM((4, V, FACE), F32), pltpu.VMEM((16, V, FACE), F32),
            pltpu.VMEM((16, FACE, FACE), F32), pltpu.SMEM((2, 4), jnp.int32), pltpu.SMEM((2, 4), jnp.int32),
            pltpu.SMEM((1,), jnp.int32),
            sems(4, 4), sems(4), sems(5, 2), sems(5, 2), sems(5, 2), sems(5, 4), sems(2), sems(2),
            sems(2, 4), sems(4), sems(4), sems(4), sems(4), sems(4), sems(4), sems(2), sems(4), sems(4), sems(2), sems(2),
        ],
        compiler_params=pltpu.CompilerParams(
            collective_id=0, has_side_effects=True, vmem_limit_bytes=60 * 2**20
        ),
        cost_estimate=pl.CostEstimate(flops=10**10, bytes_accessed=10**7, transcendentals=0),
    )(rhs, diag, lower, upper, proj, intersections.T, index.T, angle)
    return result, mortar.reshape(1, LINES, V * FACE)


def solution(mesh):
    line = P("theta", "axial", None, None)
    return jax.shard_map(
        local,
        mesh=mesh,
        in_specs=(line, line, line, line, P(), P("theta", None), P("theta", None), P()),
        out_specs=(line, P("axial", "theta", None)),
        check_vma=False,
    )
```
